256 devices in a mesh: fsdp: 32 (over x, y, core), rep: 8 (over z).
Axes of the slice: x: 4, y: 4, z: 8, core: 2. Of those that a mesh axis runs over, the one named last changes fastest.
Arguments:
- gradient: bfloat16 [32, 1024, 1024], P(None, 'fsdp'), may hold values from -6 to 6
- block_owner: int32 [32], replicated, may hold values from 0 to 31, as said below
- block_slot: int32 [32], replicated, may hold values from 0 to 2
- left_state: float32 [32, 3, 1024, 1024], P('fsdp', None, 'rep'), may hold values from -6 to 6
- right_state: float32 [32, 3, 1024, 1024], P('fsdp', None, None, 'rep'), may hold values from -6 to 6
- left_root: bfloat16 [32, 3, 1024, 1024], P('fsdp', None, 'rep'), may hold values from -0.2 to 1.4
- right_root: bfloat16 [32, 3, 1024, 1024], P('fsdp', None, None, 'rep'), may hold values from -0.2 to 1.4
Outputs:
- update: bfloat16 [32, 1024, 1024], P(None, 'fsdp')
- left_factor: float32 [32, 3, 1024, 1024], P('fsdp', None, 'rep')
- right_factor: float32 [32, 3, 1024, 1024], P('fsdp', None, None, 'rep')
The draws below stay inside these ranges and needn't reach their ends.
Inputs may be any that keep to these rules, and one draw needn't show every extreme that they name: The pairs (block_owner[i], block_slot[i]) are distinct; some owner holds blocks in all 3 of its slots.
All inputs are finite; a program needn't handle non-finite values.
Results may differ from the reference program's by a relative error of at most 0.0049.
Values may be sent and summed in bfloat16 or wider, within the bound.
No kernel may reach another device: no remote copies, remote signals or barrier semaphores. Data moves between devices by JAX's collectives and lax.ppermute only.
A program may use at most 128 MiB of HBM per device.

```python
import math
import jax
import jax.numpy as jnp
from jax import lax

BLOCK = 1024
SLOTS = 3
NBLOCKS = 32
N_FSDP = 32


def placement(key):
    key_first, key_second = jax.random.split(key)
    total = N_FSDP * SLOTS
    shuffled = jax.random.permutation(key_first, total)
    crowded = shuffled[0] // SLOTS
    ranking = jax.random.permutation(key_second, total)
    position = jnp.arange(total)
    scores = ranking + jnp.where(position // SLOTS == crowded, 0, total)
    chosen = jnp.argsort(scores)[:NBLOCKS]
    return (chosen // SLOTS, chosen % SLOTS)


def draw_block_owner(key, part):
    return placement(key)[0].astype(jnp.int32)


def draw_block_slot(key, part):
    return placement(key)[1].astype(jnp.int32)


def draw_gradient(key, part):
    key = jax.random.fold_in(key, 11)
    key_noise = jax.random.fold_in(key, 0)
    noise = jax.random.truncated_normal(key_noise, -6.0, 6.0, (NBLOCKS, BLOCK, BLOCK), jnp.float32)
    values = 0.3 * noise
    return values.astype(jnp.bfloat16)


def off_diagonal(key_off, shape):
    cutoff = min(6.0, 0.15 * math.sqrt(BLOCK) / 0.7)
    return jax.random.truncated_normal(key_off, -cutoff, cutoff, shape, jnp.float32) * (0.7 / math.sqrt(BLOCK))


def draw_left_root(key, part):
    key = jax.random.fold_in(key, 21)
    key_diag, key_off = jax.random.split(key)
    shape = (N_FSDP, SLOTS, BLOCK, BLOCK)
    diagonal = jax.random.uniform(key_diag, (N_FSDP, SLOTS, BLOCK, 1), jnp.float32, 0.6, 1.4)
    off_part = off_diagonal(key_off, shape)
    row_ids = jax.lax.broadcasted_iota(jnp.int32, (BLOCK, BLOCK), 0)
    col_ids = jax.lax.broadcasted_iota(jnp.int32, (BLOCK, BLOCK), 1)
    return jnp.where(row_ids == col_ids, diagonal, off_part).astype(jnp.bfloat16)


def draw_right_root(key, part):
    key = jax.random.fold_in(key, 31)
    key_diag, key_off = jax.random.split(key)
    shape = (N_FSDP, SLOTS, BLOCK, BLOCK)
    diagonal = jax.random.uniform(key_diag, (N_FSDP, SLOTS, 1, BLOCK), jnp.float32, 0.6, 1.4)
    off_part = off_diagonal(key_off, shape)
    row_ids = jax.lax.broadcasted_iota(jnp.int32, (BLOCK, BLOCK), 0)
    col_ids = jax.lax.broadcasted_iota(jnp.int32, (BLOCK, BLOCK), 1)
    return jnp.where(row_ids == col_ids, diagonal, off_part).astype(jnp.bfloat16)


def block_scale(key, shape, cuts, smallest, high):
    level = 1.0
    for dim, blocks in cuts:
        heights = jax.random.uniform(jax.random.fold_in(jax.random.fold_in(key, 6), dim), (blocks,), jnp.float32, smallest / len(cuts), high / len(cuts))
        level = level * jnp.repeat(jnp.exp(heights), shape[dim] // blocks).reshape((-1,) + (1,) * (len(shape) - 1 - dim))
    return level


def scatter_about(rng, shape, scale, most, shards=(), held_as=jnp.bfloat16):
    array = scale * jax.random.normal(rng, shape, jnp.float32)
    if shards:
        array = array * block_scale(rng, shape, shards, -0.22, 0.18)
    return jnp.clip(array, -most, most).astype(held_as)


def setup_inputs(seed: int = 0) -> dict:
    key_list = jax.random.split(jax.random.key(seed), 8)
    gradient = draw_gradient(jax.random.fold_in(key_list[7], 71), 0)
    block_owner = draw_block_owner(jax.random.fold_in(key_list[7], 71), 0)
    block_slot = draw_block_slot(jax.random.fold_in(key_list[7], 71), 0)
    left_state = scatter_about(key_list[3], (N_FSDP, SLOTS, BLOCK, BLOCK), 1.0, 6.0, ((0, 32), (2, 8)), jnp.float32)
    right_state = scatter_about(key_list[4], (N_FSDP, SLOTS, BLOCK, BLOCK), 1.0, 6.0, ((0, 32), (3, 8)), jnp.float32)
    left_root = draw_left_root(jax.random.fold_in(key_list[7], 71), 0)
    right_root = draw_right_root(jax.random.fold_in(key_list[7], 71), 0)
    return dict(gradient=gradient, block_owner=block_owner, block_slot=block_slot, left_state=left_state, right_state=right_state, left_root=left_root, right_root=right_root)


decay_rate = 0.95
epsilon = 1e-06

def reference(gradient, block_owner, block_slot, left_state, right_state, left_root, right_root):
    block_count = gradient.shape[0]
    positions = N_FSDP * SLOTS
    flat_index = (block_owner * SLOTS + block_slot).astype(jnp.int32)
    matches = flat_index[None, :] == jnp.arange(positions, dtype=jnp.int32)[:, None]
    occupied = jnp.any(matches, axis=1)
    sources = lax.optimization_barrier(jnp.sum(jnp.where(matches, jnp.arange(block_count, dtype=jnp.int32)[None, :], 0), axis=1)).astype(jnp.int32)
    left_flat = left_state.reshape(positions, BLOCK, BLOCK)
    right_flat = right_state.reshape(positions, BLOCK, BLOCK)
    lroot_flat = left_root.reshape(positions, BLOCK, BLOCK)
    rroot_flat = right_root.reshape(positions, BLOCK, BLOCK)

    def factors(position):
        block_grad = gradient[sources[position]].astype(jnp.float32) * occupied[position].astype(jnp.float32)
        left_new = decay_rate * left_flat[position] + (1.0 - decay_rate) * jnp.dot(block_grad, block_grad.T, precision=lax.Precision.HIGHEST)
        right_new = decay_rate * right_flat[position] + (1.0 - decay_rate) * jnp.dot(block_grad.T, block_grad, precision=lax.Precision.HIGHEST)
        return (left_new, right_new)
    left_factor, right_factor = lax.map(factors, jnp.arange(positions, dtype=jnp.int32))

    def precondition(block):
        block_grad = gradient[block]
        where_slot = flat_index[block]
        rooted = jnp.dot(block_grad, rroot_flat[where_slot], preferred_element_type=jnp.float32).astype(jnp.bfloat16)
        precond = jnp.dot(lroot_flat[where_slot], rooted, preferred_element_type=jnp.float32)
        grad_squares = jnp.sum(jnp.square(block_grad.astype(jnp.float32)))
        pre_squares = jnp.sum(precond * precond)
        graft_scale = jnp.sqrt(grad_squares) / jnp.sqrt(pre_squares + epsilon)
        return (precond * graft_scale).astype(jnp.bfloat16)
    update = lax.map(precondition, jnp.arange(block_count, dtype=jnp.int32))
    return (update, left_factor.reshape(N_FSDP, SLOTS, BLOCK, BLOCK), right_factor.reshape(N_FSDP, SLOTS, BLOCK, BLOCK))
```

```python
import jax
import jax.numpy as jnp
from jax import lax
from jax.experimental import pallas as pl
from jax.experimental.pallas import tpu as pltpu
from jax.sharding import PartitionSpec as P

decay_rate = 0.95
epsilon = 1e-06

F32 = jnp.float32
BF16 = jnp.bfloat16
LANES = 128
STRIDE = 8
VMEM_LIMIT = 48 * 1024 * 1024


def split_three(value):
    high = value.astype(BF16).astype(F32)
    rest = value - high
    middle = rest.astype(BF16).astype(F32)
    return high, middle, (rest - middle).astype(BF16).astype(F32)


def update_kernel(rep_ref, blocks_ref, left_ref, right_ref, out_ref, sums_ref):
    slot = pl.program_id(0)
    slots = pl.num_programs(0)
    pieces, rows, order = blocks_ref.shape
    width = right_ref.shape[1]
    block = blocks_ref[...].reshape(pieces * rows, order)
    rooted = jnp.dot(block, right_ref[...], preferred_element_type=F32).astype(BF16)
    precond = jnp.dot(left_ref[...], rooted, preferred_element_type=F32)
    start = pl.multiple_of(slot * rows, rows)
    out_ref[:, pl.ds(start, rows), :] = precond.astype(BF16).reshape(pieces, rows, width)
    columns = pl.multiple_of(rep_ref[0] * width, width)
    own = blocks_ref[:, :, pl.ds(columns, width)].astype(F32)
    lane = lax.broadcasted_iota(jnp.int32, sums_ref.shape, 1)

    @pl.when(slot == 0)
    def _():
        sums_ref[...] = jnp.zeros_like(sums_ref)

    total = sums_ref[...]
    parts = split_three(jnp.sum(precond * precond, keepdims=True))
    parts += split_three(jnp.sum(own * own, keepdims=True).reshape(1, 1))
    for index, part in enumerate(parts):
        total = jnp.where(lane == slot * STRIDE + index, part, total)
    sums_ref[...] = total

    @pl.when(slot == slots - 1)
    def _():
        tail = sums_ref[...].astype(BF16)
        out_ref[:, slots * rows :, :] = jnp.broadcast_to(tail, (pieces,) + tail.shape)


def precondition(rep, blocks, left, right):
    pieces, slots, rows, order = blocks.shape
    width = right.shape[-1]
    tail = 16
    return pl.pallas_call(
        update_kernel,
        grid_spec=pltpu.PrefetchScalarGridSpec(
            num_scalar_prefetch=1,
            grid=(slots,),
            in_specs=[
                pl.BlockSpec((pieces, None, rows, order), lambda k, rep: (0, k, 0, 0)),
                pl.BlockSpec((None, order, order), lambda k, rep: (k, 0, 0)),
                pl.BlockSpec((None, order, width), lambda k, rep: (k, 0, 0)),
            ],
            out_specs=pl.BlockSpec(
                (pieces, slots * rows + tail, width), lambda k, rep: (0, 0, 0)
            ),
            scratch_shapes=[pltpu.VMEM((tail, width), F32)],
        ),
        out_shape=jax.ShapeDtypeStruct((pieces, slots * rows + tail, width), BF16),
        compiler_params=pltpu.CompilerParams(vmem_limit_bytes=VMEM_LIMIT),
        cost_estimate=pl.CostEstimate(
            flops=slots * 4 * order * order * width,
            bytes_accessed=slots * 4 * order * order,
            transcendentals=0,
        ),
        name="precondition",
    )(rep, blocks, left, right)


def select_kernel(owner_ref, slot_ref, arrived_ref, out_ref):
    count, rows, width = out_ref.shape
    count -= 1
    slots_rows = arrived_ref.shape[1] - 16
    line = lax.broadcasted_iota(jnp.int32, (rows, width), 0)
    sums = jnp.zeros((rows, width), F32)
    for index in range(count):
        owner = owner_ref[index]
        start = pl.multiple_of(slot_ref[index] * rows, rows)
        out_ref[index] = arrived_ref[owner, pl.ds(start, rows), :]
        tail = arrived_ref[owner, slots_rows : slots_rows + 16, :].astype(F32)
        sums = jnp.where(line == index, jnp.concatenate([tail, tail], axis=0), sums)
    out_ref[count] = sums.astype(BF16)


def select(owner, slot, arrived):
    count, rows = owner.shape[0], (arrived.shape[1] - 16) // 3
    width = arrived.shape[2]
    return pl.pallas_call(
        select_kernel,
        grid_spec=pltpu.PrefetchScalarGridSpec(
            num_scalar_prefetch=2,
            grid=(1,),
            in_specs=[pl.BlockSpec(arrived.shape, lambda i, o, s: (0, 0, 0))],
            out_specs=pl.BlockSpec((count + 1, rows, width), lambda i, o, s: (0, 0, 0)),
        ),
        out_shape=jax.ShapeDtypeStruct((count + 1, rows, width), BF16),
        compiler_params=pltpu.CompilerParams(vmem_limit_bytes=VMEM_LIMIT),
        name="select",
    )(owner, slot, arrived)


def finish_kernel(rep_ref, slot_ref, *refs):
    out_ref, scale_ref = refs[-2:]
    shares = refs[:-2]
    count, rows, order = out_ref.shape
    width = shares[0].shape[2]
    half = shares[7].shape[0]
    replicas = order // width
    sums = shares[8][count - half].astype(F32)
    for share in shares[:7]:
        sums += share[count].astype(F32)
    lane = lax.broadcasted_iota(jnp.int32, (rows, width), 1) - slot_ref[...] * STRIDE
    pre = jnp.sum(jnp.where((lane >= 0) & (lane < 3), sums, 0.0), axis=1, keepdims=True)
    grad = jnp.sum(jnp.where((lane >= 3) & (lane < 6), sums, 0.0), axis=1, keepdims=True)
    scale = jnp.sqrt(grad) / jnp.sqrt(pre + epsilon)
    scale_ref[...] = jnp.broadcast_to(scale, (rows, width))

    def place(index, share, column):
        factor = scale_ref[pl.ds(index, 1), :]
        start = pl.multiple_of(column * width, width)
        out_ref[index, :, pl.ds(start, width)] = (share.astype(F32) * factor).astype(BF16)

    distances = (0, 1, 2, 3, -1, -2, -3)
    for index in range(count):
        for share, distance in zip(shares[:7], distances):
            place(index, share[index], lax.rem(rep_ref[0] - distance + replicas, replicas))
        far = lax.rem(rep_ref[0] + replicas // 2, replicas)
        share = shares[7][index] if index < half else shares[8][index - half]
        place(index, share, far)


def finish(rep, slot, shares, count, rows, order):
    slot_rows = jnp.broadcast_to(slot[:, None], (count, LANES))
    return pl.pallas_call(
        finish_kernel,
        in_specs=[pl.BlockSpec(memory_space=pltpu.SMEM)]
        + [pl.BlockSpec(memory_space=pltpu.VMEM)] * (1 + len(shares)),
        out_specs=pl.BlockSpec(memory_space=pltpu.VMEM),
        out_shape=jax.ShapeDtypeStruct((count, rows, order), BF16),
        scratch_shapes=[pltpu.VMEM((count, LANES), F32)],
        compiler_params=pltpu.CompilerParams(vmem_limit_bytes=VMEM_LIMIT),
        name="finish",
    )(rep, slot_rows, *shares)


def factor_kernel(rep_ref, occupied_ref, blocks_ref, left_ref, right_ref, left_out, right_out):
    slot = pl.program_id(0)
    pieces, rows, order = blocks_ref.shape
    width = right_ref.shape[1]
    rep = rep_ref[0]
    weight = (1.0 - decay_rate) * occupied_ref[slot].astype(F32)
    block = blocks_ref[...].reshape(pieces * rows, order)
    share = width // rows
    own_rows = blocks_ref[pl.ds(rep * share, share)].reshape(width, order)
    columns = pl.multiple_of(rep * width, width)
    own_columns = blocks_ref[:, :, pl.ds(columns, width)].reshape(order, width)
    left = lax.dot_general(
        own_rows, block, (((1,), (1,)), ((), ())), preferred_element_type=F32
    )
    left_out[...] = decay_rate * left_ref[...] + weight * left
    right = jnp.dot(own_columns.T, block, preferred_element_type=F32).T
    right_out[...] = decay_rate * right_ref[...] + weight * right


def factors(rep, occupied, blocks, left, right):
    pieces, slots, rows, order = blocks.shape
    width = right.shape[-1]
    left_spec = pl.BlockSpec((None, None, width, order), lambda k, a, b: (0, k, 0, 0))
    right_spec = pl.BlockSpec((None, None, order, width), lambda k, a, b: (0, k, 0, 0))
    return pl.pallas_call(
        factor_kernel,
        grid_spec=pltpu.PrefetchScalarGridSpec(
            num_scalar_prefetch=2,
            grid=(slots,),
            in_specs=[
                pl.BlockSpec((pieces, None, rows, order), lambda k, a, b: (0, k, 0, 0)),
                left_spec,
                right_spec,
            ],
            out_specs=[left_spec, right_spec],
        ),
        out_shape=[
            jax.ShapeDtypeStruct(left.shape, F32),
            jax.ShapeDtypeStruct(right.shape, F32),
        ],
        compiler_params=pltpu.CompilerParams(vmem_limit_bytes=VMEM_LIMIT),
        cost_estimate=pl.CostEstimate(
            flops=slots * 4 * order * order * width,
            bytes_accessed=slots * 6 * order * order,
            transcendentals=0,
        ),
        name="factors",
    )(rep, occupied, blocks, left, right)


def ring_gather(share, axis):
    size = lax.axis_size(axis)
    half = share.shape[0] // 2

    def shift(value, by):
        return lax.ppermute(value, axis, [(i, (i + by) % size) for i in range(size)])

    up, down = [share], [share]
    for _ in range(size // 2 - 1):
        up.append(shift(up[-1], 1))
        down.append(shift(down[-1], -1))
    far_up = shift(up[-1][:half], 1)
    far_down = shift(down[-1][half:], -1)
    return up + down[1:] + [far_up, far_down]


def local(gradient, block_owner, block_slot, left_state, right_state, left_root, right_root):
    owners_count = lax.axis_size("fsdp")
    block_count, row_share, block_order = gradient.shape
    slot_count = left_state.shape[1]
    rep = lax.axis_index("rep").astype(jnp.int32).reshape(1)
    positions = owners_count * slot_count
    flat_index = block_owner * slot_count + block_slot
    matches = flat_index[None, :] == jnp.arange(positions, dtype=jnp.int32)[:, None]
    occupied = jnp.any(matches, axis=1).astype(jnp.int32)
    sources = jnp.sum(
        jnp.where(matches, jnp.arange(block_count, dtype=jnp.int32)[None, :], 0), axis=1
    )
    mine = lax.dynamic_slice_in_dim(
        occupied, lax.axis_index("fsdp") * slot_count, slot_count, 0
    )
    left_full = lax.all_gather(left_root[0], "rep", axis=1, tiled=True)
    packed = gradient.at[sources].get(mode="promise_in_bounds")
    packed = packed.reshape(owners_count, slot_count, row_share, block_order)
    blocks = lax.all_to_all(packed, "fsdp", split_axis=0, concat_axis=0, tiled=True)
    outgoing = precondition(rep, blocks, left_full, right_root[0])
    arrived = lax.all_to_all(outgoing, "fsdp", split_axis=0, concat_axis=0, tiled=True)
    named = select(block_owner, block_slot, arrived)
    left_factor, right_factor = factors(rep, mine, blocks, left_state, right_state)
    shares = ring_gather(named, "rep")
    update = finish(rep, block_slot, shares, block_count, row_share, block_order)
    return (update, left_factor, right_factor)


def solution(mesh):
    in_specs = (
        P(None, "fsdp", None),
        P(),
        P(),
        P("fsdp", None, "rep", None),
        P("fsdp", None, None, "rep"),
        P("fsdp", None, "rep", None),
        P("fsdp", None, None, "rep"),
    )
    out_specs = (P(None, "fsdp", None), P("fsdp", None, "rep", None), P("fsdp", None, None, "rep"))
    return jax.shard_map(local, mesh=mesh, in_specs=in_specs, out_specs=out_specs, check_vma=False)
```

```python
import jax
import jax.numpy as jnp
from jax import lax
from jax.experimental import pallas as pl
from jax.experimental.pallas import tpu as pltpu
from jax.sharding import PartitionSpec as P

decay_rate = 0.95
epsilon = 1e-06

F32 = jnp.float32
BF16 = jnp.bfloat16
ROWS = 32
TILE = 16
LANES = 128
VMEM_LIMIT = 48 * 1024 * 1024
DISTANCES = (0, 1, 2, 3, -1, -2, -3)


def params():
    return pltpu.CompilerParams(vmem_limit_bytes=VMEM_LIMIT)


def whole(shape):
    return pl.BlockSpec(shape, lambda *_: (0,) * len(shape))


def row_piece(index):
    per_line = 1024 // (2 * LANES)
    return TILE * (index // per_line), 2 * LANES * (index % per_line)


def split_three(value):
    high = value.astype(BF16).astype(F32)
    rest = value - high
    middle = rest.astype(BF16).astype(F32)
    return high, middle, (rest - middle).astype(BF16).astype(F32)


def pack_kernel(left_ref, right_ref, out_ref):
    for slot in range(left_ref.shape[0]):
        base = 2 * ROWS * slot
        for index in range(out_ref.shape[0]):
            row, column = row_piece(index)
            rows = pl.ds(row, TILE)
            out_ref[index, base : base + TILE] = left_ref[slot, rows, column : column + LANES]
            out_ref[index, base + TILE : base + ROWS] = left_ref[
                slot, rows, column + LANES : column + 2 * LANES
            ]
            out_ref[index, base + ROWS : base + 2 * ROWS] = right_ref[
                slot, ROWS * index : ROWS * (index + 1)
            ]


def pack(left, right, pieces):
    return pl.pallas_call(
        pack_kernel,
        out_shape=jax.ShapeDtypeStruct((pieces, left.shape[0] * 2 * ROWS, LANES), BF16),
        compiler_params=params(),
        name="pack",
    )(left, right)


def route_kernel(owner_ref, slot_ref, arrived_ref, out_ref):
    for index in range(out_ref.shape[0]):
        start = pl.multiple_of(slot_ref[index] * (2 * ROWS), 2 * ROWS)
        out_ref[index] = arrived_ref[owner_ref[index], pl.ds(start, 2 * ROWS), :]


def route(owner, slot, arrived):
    shape = (owner.shape[0], 2 * ROWS, LANES)
    return pl.pallas_call(
        route_kernel,
        grid_spec=pltpu.PrefetchScalarGridSpec(
            num_scalar_prefetch=2,
            grid=(1,),
            in_specs=[whole(arrived.shape)],
            out_specs=whole(shape),
        ),
        out_shape=jax.ShapeDtypeStruct(shape, BF16),
        compiler_params=params(),
        name="route",
    )(owner, slot, arrived)


def block_kernel(rep_ref, block_ref, roots_ref, *refs):
    shares, (out_ref, left_ref) = refs[:-2], refs[-2:]
    pieces, rows, order = block_ref.shape
    width = LANES
    replicas = order // width
    rep = rep_ref[0]
    half = shares[7].shape[0]

    def place(index, share, start):
        row, column = row_piece(index)
        lines = pl.ds(pl.multiple_of(start + row, TILE), TILE)
        left_ref[lines, column : column + width] = share[:TILE]
        left_ref[lines, column + width : column + 2 * width] = share[TILE:]

    for share, distance in zip(shares[:7], DISTANCES):
        start = lax.rem(rep - distance + replicas, replicas) * width
        for index in range(pieces):
            place(index, share[index], start)
    start = lax.rem(rep + replicas // 2, replicas) * width
    for index in range(pieces):
        share = shares[7][index] if index < half else shares[8][index - half]
        place(index, share, start)

    block = block_ref[...].reshape(order, order)
    right_root = roots_ref[:, ROWS:, :].reshape(order, width)
    rooted = jnp.dot(block, right_root, preferred_element_type=F32).astype(BF16)
    precond = jnp.dot(left_ref[...], rooted, preferred_element_type=F32)
    out_ref[:, :ROWS, :] = precond.astype(BF16).reshape(pieces, rows, width)

    columns = pl.multiple_of(rep * width, width)
    own_columns = block_ref[:, :, pl.ds(columns, width)].reshape(order, width)
    own_rows = block_ref[pl.ds(rep * (width // rows), width // rows)].reshape(width, order)
    left = lax.dot_general(
        own_rows, block, (((1,), (1,)), ((), ())), preferred_element_type=F32
    ).astype(BF16)
    for index in range(pieces):
        row, column = row_piece(index)
        out_ref[index, ROWS : ROWS + TILE] = left[row : row + TILE, column : column + width]
        out_ref[index, ROWS + TILE : 2 * ROWS] = left[
            row : row + TILE, column + width : column + 2 * width
        ]
    right = jnp.dot(own_columns.T, block, preferred_element_type=F32).T
    out_ref[:, 2 * ROWS : 3 * ROWS, :] = right.astype(BF16).reshape(pieces, rows, width)

    own = own_columns.astype(F32)
    lane = lax.broadcasted_iota(jnp.int32, (TILE, width), 1)
    total = jnp.zeros((TILE, width), F32)
    parts = split_three(jnp.sum(precond * precond, keepdims=True))
    parts += split_three(jnp.sum(own * own, keepdims=True))
    for index, part in enumerate(parts):
        total = jnp.where(lane == index, part, total)
    out_ref[:, 3 * ROWS :, :] = jnp.broadcast_to(total.astype(BF16), (pieces, TILE, width))


def block_shares(rep, block, roots, shares):
    pieces, _, order = block.shape
    out = (pieces, 3 * ROWS + TILE, LANES)
    return pl.pallas_call(
        block_kernel,
        in_specs=[pl.BlockSpec(memory_space=pltpu.SMEM)]
        + [pl.BlockSpec(memory_space=pltpu.VMEM)] * (2 + len(shares)),
        out_specs=pl.BlockSpec(memory_space=pltpu.VMEM),
        out_shape=jax.ShapeDtypeStruct(out, BF16),
        scratch_shapes=[pltpu.VMEM((order, order), BF16)],
        compiler_params=params(),
        name="block_shares",
    )(rep, block, roots, *shares)


def deal_kernel(sources_ref, arrived_ref, update_ref, products_ref):
    count = arrived_ref.shape[0]
    line = lax.broadcasted_iota(jnp.int32, (ROWS, LANES), 0)
    sums = jnp.zeros((ROWS, LANES), F32)
    for index in range(count):
        update_ref[index] = arrived_ref[index, :ROWS, :]
        tail = arrived_ref[index, 3 * ROWS :, :].astype(F32)
        sums = jnp.where(line == index, jnp.concatenate([tail, tail], axis=0), sums)
    update_ref[count] = sums.astype(BF16)
    slots = products_ref.shape[1] // (2 * ROWS)
    for owner in range(products_ref.shape[0]):
        for slot in range(slots):
            source = sources_ref[owner * slots + slot]
            products_ref[owner, 2 * ROWS * slot : 2 * ROWS * (slot + 1)] = arrived_ref[
                source, ROWS : 3 * ROWS, :
            ]


def deal(sources, arrived, owners):
    count = arrived.shape[0]
    shapes = [
        (count + 1, ROWS, LANES),
        (owners, sources.shape[0] // owners * 2 * ROWS, LANES),
    ]
    return pl.pallas_call(
        deal_kernel,
        grid_spec=pltpu.PrefetchScalarGridSpec(
            num_scalar_prefetch=1,
            grid=(1,),
            in_specs=[whole(arrived.shape)],
            out_specs=[whole(shape) for shape in shapes],
        ),
        out_shape=[jax.ShapeDtypeStruct(shape, BF16) for shape in shapes],
        compiler_params=params(),
        name="deal",
    )(sources, arrived)


def finish_kernel(rep_ref, *refs):
    shares, (out_ref, scale_ref) = refs[:-2], refs[-2:]
    count, rows, order = out_ref.shape
    width = LANES
    half = shares[7].shape[0]
    replicas = order // width
    sums = shares[8][count - half].astype(F32)
    for share in shares[:7]:
        sums += share[count].astype(F32)
    lane = lax.broadcasted_iota(jnp.int32, (rows, width), 1)
    pre = jnp.sum(jnp.where(lane < 3, sums, 0.0), axis=1, keepdims=True)
    grad = jnp.sum(jnp.where((lane >= 3) & (lane < 6), sums, 0.0), axis=1, keepdims=True)
    scale = jnp.sqrt(grad) / jnp.sqrt(pre + epsilon)
    scale_ref[...] = jnp.broadcast_to(scale, (rows, width))

    def place(index, share, column):
        factor = scale_ref[pl.ds(index, 1), :]
        start = pl.multiple_of(column * width, width)
        out_ref[index, :, pl.ds(start, width)] = (share.astype(F32) * factor).astype(BF16)

    for index in range(count):
        for share, distance in zip(shares[:7], DISTANCES):
            place(index, share[index], lax.rem(rep_ref[0] - distance + replicas, replicas))
        far = lax.rem(rep_ref[0] + replicas // 2, replicas)
        share = shares[7][index] if index < half else shares[8][index - half]
        place(index, share, far)


def finish(rep, shares, count, rows, order):
    return pl.pallas_call(
        finish_kernel,
        in_specs=[pl.BlockSpec(memory_space=pltpu.SMEM)]
        + [pl.BlockSpec(memory_space=pltpu.VMEM)] * len(shares),
        out_specs=pl.BlockSpec(memory_space=pltpu.VMEM),
        out_shape=jax.ShapeDtypeStruct((count, rows, order), BF16),
        scratch_shapes=[pltpu.VMEM((count, LANES), F32)],
        compiler_params=params(),
        name="finish",
    )(rep, *shares)


def factor_kernel(occupied_ref, products_ref, left_ref, right_ref, left_out, right_out):
    pieces = products_ref.shape[0]
    order, width = right_ref.shape
    occupied = occupied_ref[pl.program_id(0)]
    weight = (1.0 - decay_rate) * occupied.astype(F32)
    for index in range(pieces):
        row, column = row_piece(index)
        piece = products_ref[index].astype(F32)
        for part in range(2):
            at = (pl.ds(row, TILE), pl.ds(column + part * width, width))
            product = piece[part * TILE : (part + 1) * TILE]
            left_out[at] = decay_rate * left_ref[at] + weight * product
        at = pl.ds(ROWS * index, ROWS)
        right_out[at, :] = decay_rate * right_ref[at, :] + weight * piece[ROWS:]


def factors(occupied, products, left, right):
    slots, width, order = left.shape[1:]
    left_spec = pl.BlockSpec((None, None, width, order), lambda k, a: (0, k, 0, 0))
    right_spec = pl.BlockSpec((None, None, order, width), lambda k, a: (0, k, 0, 0))
    pieces = products.shape[0]
    return pl.pallas_call(
        factor_kernel,
        grid_spec=pltpu.PrefetchScalarGridSpec(
            num_scalar_prefetch=1,
            grid=(slots,),
            in_specs=[
                pl.BlockSpec((pieces, 2 * ROWS, LANES), lambda k, a: (0, k, 0)),
                left_spec,
                right_spec,
            ],
            out_specs=[left_spec, right_spec],
        ),
        out_shape=[
            jax.ShapeDtypeStruct(left.shape, F32),
            jax.ShapeDtypeStruct(right.shape, F32),
        ],
        compiler_params=params(),
        name="factors",
    )(occupied, products, left, right)


def ring_gather(share, axis):
    size = lax.axis_size(axis)
    half = share.shape[0] // 2

    def shift(value, by):
        return lax.ppermute(value, axis, [(i, (i + by) % size) for i in range(size)])

    up, down = [share], [share]
    for _ in range(size // 2 - 1):
        up.append(shift(up[-1], 1))
        down.append(shift(down[-1], -1))
    far_up = shift(up[-1][:half], 1)
    far_down = shift(down[-1][half:], -1)
    return up + down[1:] + [far_up, far_down]


def exchange(value):
    return lax.all_to_all(value, "fsdp", split_axis=0, concat_axis=0, tiled=True)


def local(gradient, block_owner, block_slot, left_state, right_state, left_root, right_root):
    owners = lax.axis_size("fsdp")
    count, rows, order = gradient.shape
    slots = left_state.shape[1]
    rep = lax.axis_index("rep").astype(jnp.int32).reshape(1)
    flat_index = block_owner * slots + block_slot
    matches = flat_index[None, :] == jnp.arange(owners * slots, dtype=jnp.int32)[:, None]
    occupied = jnp.any(matches, axis=1).astype(jnp.int32)
    numbers = jnp.arange(count, dtype=jnp.int32)
    sources = jnp.sum(jnp.where(matches, numbers[None, :], 0), axis=1)
    mine = lax.dynamic_slice_in_dim(occupied, lax.axis_index("fsdp") * slots, slots, 0)

    spread = exchange(pack(left_root[0], right_root[0], owners))
    roots = exchange(route(block_owner, block_slot, spread))
    roots, gradient = lax.optimization_barrier((roots, gradient))
    left_shares = ring_gather(roots[:, :ROWS, :], "rep")
    block = exchange(gradient)

    arrived = exchange(block_shares(rep, block, roots, left_shares))
    named, products = deal(sources, arrived, owners)
    products = exchange(products)
    update = finish(rep, ring_gather(named, "rep"), count, rows, order)
    left_factor, right_factor = factors(mine, products, left_state, right_state)
    return (update, left_factor, right_factor)


def solution(mesh):
    in_specs = (
        P(None, "fsdp", None),
        P(),
        P(),
        P("fsdp", None, "rep", None),
        P("fsdp", None, None, "rep"),
        P("fsdp", None, "rep", None),
        P("fsdp", None, None, "rep"),
    )
    out_specs = (P(None, "fsdp", None), P("fsdp", None, "rep", None), P("fsdp", None, None, "rep"))
    return jax.shard_map(local, mesh=mesh, in_specs=in_specs, out_specs=out_specs, check_vma=False)
```

```python
import jax
import jax.numpy as jnp
from jax import lax
from jax.experimental import pallas as pl
from jax.experimental.pallas import tpu as pltpu
from jax.sharding import PartitionSpec as P

decay_rate = 0.95
epsilon = 1e-06

F32 = jnp.float32
BF16 = jnp.bfloat16
ROWS = 32
TILE = 16
LANES = 128
DISTANCES = (0, 1, 2, 3, -1, -2, -3)


def params(mebibytes):
    return pltpu.CompilerParams(vmem_limit_bytes=mebibytes * 1024 * 1024)


def in_hbm(*arrays):
    return [pltpu.with_memory_space_constraint(array, pltpu.HBM) for array in arrays]


def cost(flops, accessed):
    return pl.CostEstimate(flops=flops, bytes_accessed=accessed, transcendentals=0)


def whole(shape):
    return pl.BlockSpec(shape, lambda *_: (0,) * len(shape))


def row_piece(index):
    per_line = 1024 // (2 * LANES)
    return TILE * (index // per_line), 2 * LANES * (index % per_line)


def split_three(value):
    high = value.astype(BF16).astype(F32)
    rest = value - high
    middle = rest.astype(BF16).astype(F32)
    return high, middle, (rest - middle).astype(BF16).astype(F32)


SOURCE = 0
HOME_BLOCK = 96
HOME_ORIGIN = 128
SPARE_HOME = 160
PLAN = 256


def plan_kernel(owner_ref, slot_ref, plan_ref, list_ref):
    owners = HOME_ORIGIN - HOME_BLOCK
    slots = (HOME_BLOCK - SOURCE) // owners

    def clear(index, carry):
        plan_ref[SOURCE + index] = -1
        return carry

    def clear_spare(index, carry):
        plan_ref[SPARE_HOME + index] = 0
        return carry

    def enter(index, carry):
        plan_ref[SOURCE + owner_ref[index] * slots + slot_ref[index]] = index
        return carry

    def walk(owner, carry):
        spare, idle = carry
        count = 0
        for slot in range(slots):
            block = plan_ref[SOURCE + owner * slots + slot]
            named = block >= 0

            @pl.when(named & (count == 0))
            def _():
                plan_ref[HOME_BLOCK + owner] = block
                plan_ref[HOME_ORIGIN + owner] = -1

            @pl.when(named & (count > 0))
            def _():
                list_ref[0, spare] = block
                list_ref[1, spare] = owner * 2 + count - 1

            spare += (named & (count > 0)).astype(jnp.int32)
            count += named.astype(jnp.int32)

        @pl.when(count == 0)
        def _():
            list_ref[2, idle] = owner

        return spare, idle + (count == 0).astype(jnp.int32)

    def assign(index, carry):
        home = list_ref[2, index]
        origin = list_ref[1, index]
        plan_ref[HOME_BLOCK + home] = list_ref[0, index]
        plan_ref[HOME_ORIGIN + home] = origin
        plan_ref[SPARE_HOME + origin] = home
        return carry

    zero = jnp.int32(0)
    lax.fori_loop(0, owners * slots, clear, zero)
    lax.fori_loop(0, 2 * owners, clear_spare, zero)
    lax.fori_loop(0, owner_ref.shape[0], enter, zero)
    _, idle = lax.fori_loop(0, owners, walk, (zero, zero))
    lax.fori_loop(0, idle, assign, zero)


def make_plan(owner, slot):
    smem = pl.BlockSpec(memory_space=pltpu.SMEM)
    return pl.pallas_call(
        plan_kernel,
        in_specs=[smem, smem],
        out_specs=smem,
        out_shape=jax.ShapeDtypeStruct((PLAN,), jnp.int32),
        scratch_shapes=[pltpu.SMEM((3, 32), jnp.int32)],
        compiler_params=params(4),
        name="make_plan",
    )(owner, slot)


def cut(left_ref, right_ref, slot, out_ref, base):
    for index in range(out_ref.shape[0]):
        row, column = row_piece(index)
        rows = pl.ds(row, TILE)
        out_ref[index, base : base + TILE] = left_ref[slot, rows, column : column + LANES]
        out_ref[index, base + TILE : base + ROWS] = left_ref[
            slot, rows, column + LANES : column + 2 * LANES
        ]
        out_ref[index, base + ROWS : base + 2 * ROWS] = right_ref[
            slot, ROWS * index : ROWS * (index + 1)
        ]


def pack_kernel(
    place_ref, owner_hbm, slot_hbm, left_hbm, right_hbm, spare_hbm, *scratch
):
    owner_ref, slot_ref, left_ref, right_ref, spare_ref, sems = scratch
    spares = left_ref.shape[0]
    roots = []
    for spare in range(spares):
        pair = (
            pltpu.make_async_copy(left_hbm.at[spare + 1], left_ref.at[spare], sems.at[0, spare]),
            pltpu.make_async_copy(right_hbm.at[spare + 1], right_ref.at[spare], sems.at[1, spare]),
        )
        roots.append(pair)
    names = (
        pltpu.make_async_copy(owner_hbm, owner_ref, sems.at[2, 0]),
        pltpu.make_async_copy(slot_hbm, slot_ref, sems.at[2, 1]),
    )
    for copy in names + roots[1] + roots[0]:
        copy.start()
    for copy in names:
        copy.wait()

    def look(index, found):
        own = owner_ref[index] == place_ref[1]
        return found + (own & (slot_ref[index] < spares)).astype(jnp.int32)

    found = lax.fori_loop(0, owner_ref.shape[0], look, jnp.int32(0), unroll=4)
    second = jnp.where(found == spares, 0, 1)
    for copy in roots[1]:
        copy.wait()
    writes = []
    for spare in (1, 0):
        if spare == 0:
            for copy in roots[0]:
                copy.wait()
        cut(left_ref, right_ref, 1 if spare else second, spare_ref, 2 * ROWS * spare)
        part = (slice(None), pl.ds(2 * ROWS * spare, 2 * ROWS))
        copy = pltpu.make_async_copy(spare_ref.at[part], spare_hbm.at[part], sems.at[3, spare])
        copy.start()
        writes.append(copy)
    for copy in writes:
        copy.wait()


def pack(place, owner, slot, left, right, pieces):
    hbm = pl.BlockSpec(memory_space=pltpu.HBM)
    spares = left.shape[0] - 1
    shape = (pieces, spares * 2 * ROWS, LANES)
    return pl.pallas_call(
        pack_kernel,
        in_specs=[pl.BlockSpec(memory_space=pltpu.SMEM)] + [hbm] * 4,
        out_specs=hbm,
        out_shape=pltpu.HBM(shape, BF16),
        scratch_shapes=[
            pltpu.SMEM(owner.shape, jnp.int32),
            pltpu.SMEM(slot.shape, jnp.int32),
            pltpu.VMEM((spares,) + left.shape[1:], BF16),
            pltpu.VMEM((spares,) + right.shape[1:], BF16),
            pltpu.VMEM(shape, BF16),
            pltpu.SemaphoreType.DMA((4, 2)),
        ],
        compiler_params=params(8),
        name="pack",
    )(place, *in_hbm(owner, slot, left, right))


def keep_kernel(place_ref, plan_ref, left_hbm, right_hbm, kept_ref, left_ref, right_ref, sems):
    slots = left_hbm.shape[0]
    first = jnp.int32(slots - 1)
    for slot in reversed(range(slots - 1)):
        first = jnp.where(plan_ref[SOURCE + place_ref[1] * slots + slot] >= 0, slot, first)
    copies = (
        pltpu.make_async_copy(left_hbm.at[first], left_ref.at[0], sems.at[0]),
        pltpu.make_async_copy(right_hbm.at[first], right_ref.at[0], sems.at[1]),
    )
    for copy in copies:
        copy.start()
    for copy in copies:
        copy.wait()
    cut(left_ref, right_ref, 0, kept_ref, 0)


def keep(place, plan, left, right, pieces):
    smem = pl.BlockSpec(memory_space=pltpu.SMEM)
    hbm = pl.BlockSpec(memory_space=pltpu.HBM)
    return pl.pallas_call(
        keep_kernel,
        in_specs=[smem, smem, hbm, hbm],
        out_specs=pl.BlockSpec(memory_space=pltpu.VMEM),
        out_shape=jax.ShapeDtypeStruct((pieces, 2 * ROWS, LANES), BF16),
        scratch_shapes=[
            pltpu.VMEM((1,) + left.shape[1:], BF16),
            pltpu.VMEM((1,) + right.shape[1:], BF16),
            pltpu.SemaphoreType.DMA((2,)),
        ],
        compiler_params=params(8),
        name="keep",
    )(place, plan, *in_hbm(left, right))


def route_kernel(plan_ref, arrived_ref, out_hbm, sems):
    copies = []
    for home in range(out_hbm.shape[0]):
        origin = jnp.maximum(plan_ref[HOME_ORIGIN + home], 0)
        start = pl.multiple_of(lax.rem(origin, 2) * (2 * ROWS), 2 * ROWS)
        source = arrived_ref.at[lax.div(origin, 2), pl.ds(start, 2 * ROWS)]
        copies.append(pltpu.make_async_copy(source, out_hbm.at[home], sems.at[home]))
        copies[-1].start()
    for copy in copies:
        copy.wait()


def route(plan, arrived):
    homes = arrived.shape[0]
    return pl.pallas_call(
        route_kernel,
        in_specs=[
            pl.BlockSpec(memory_space=pltpu.SMEM),
            pl.BlockSpec(memory_space=pltpu.VMEM),
        ],
        out_specs=pl.BlockSpec(memory_space=pltpu.HBM),
        out_shape=pltpu.HBM((homes, 2 * ROWS, LANES), BF16),
        scratch_shapes=[pltpu.SemaphoreType.DMA((homes,))],
        compiler_params=params(8),
        name="route",
    )(plan, arrived)


def pick_kernel(place_ref, plan_ref, kept_ref, roots_ref, left_ref, both_hbm, sem):
    own = plan_ref[HOME_ORIGIN + place_ref[1]] < 0

    def take(source_ref):
        copy = pltpu.make_async_copy(source_ref, both_hbm, sem)
        copy.start()
        left_ref[...] = source_ref[:, :ROWS]
        copy.wait()

    @pl.when(own)
    def _():
        take(kept_ref)

    @pl.when(jnp.logical_not(own))
    def _():
        take(roots_ref)


def pick(place, plan, kept, roots):
    smem = pl.BlockSpec(memory_space=pltpu.SMEM)
    vmem = pl.BlockSpec(memory_space=pltpu.VMEM)
    return pl.pallas_call(
        pick_kernel,
        in_specs=[smem, smem, vmem, vmem],
        out_specs=[vmem, pl.BlockSpec(memory_space=pltpu.HBM)],
        out_shape=[
            jax.ShapeDtypeStruct((kept.shape[0], ROWS, LANES), BF16),
            pltpu.HBM(kept.shape, BF16),
        ],
        scratch_shapes=[pltpu.SemaphoreType.DMA],
        compiler_params=params(8),
        name="pick",
    )(place, plan, kept, roots)


def gather_kernel(plan_ref, gradient_ref, out_ref):
    for home in range(out_ref.shape[0]):
        out_ref[home] = gradient_ref[plan_ref[HOME_BLOCK + home]]


def gather(plan, gradient):
    return pl.pallas_call(
        gather_kernel,
        in_specs=[
            pl.BlockSpec(memory_space=pltpu.SMEM),
            pl.BlockSpec(memory_space=pltpu.VMEM),
        ],
        out_shape=jax.ShapeDtypeStruct(gradient.shape, BF16),
        compiler_params=params(8),
        name="gather",
    )(plan, gradient)


def block_kernel(rep_ref, block_hbm, both_hbm, *refs):
    shares, (out_ref, own_ref, block_ref, both_ref, left_ref, sems) = refs[:-6], refs[-6:]
    pieces, rows, order = block_ref.shape
    width = LANES
    replicas = order // width
    rep = rep_ref[0]
    half = shares[6].shape[0]
    roots = pltpu.make_async_copy(both_hbm, both_ref, sems.at[0])
    roots.start()
    parts = 4
    blocks = []
    for part in range(parts):
        lines = pl.ds(part * (pieces // parts), pieces // parts)
        copy = pltpu.make_async_copy(
            block_hbm.at[lines], block_ref.at[lines], sems.at[1 + part]
        )
        copy.start()
        blocks.append(copy)

    def place(index, share, start):
        row, column = row_piece(index)
        lines = pl.ds(pl.multiple_of(start + row, TILE), TILE)
        left_ref[lines, column : column + width] = share[:TILE]
        left_ref[lines, column + width : column + 2 * width] = share[TILE:]

    for share, distance in zip(shares[:6], DISTANCES[1:]):
        start = lax.rem(rep - distance + replicas, replicas) * width
        for index in range(pieces):
            place(index, share[index], start)
    start = lax.rem(rep + replicas // 2, replicas) * width
    for index in range(pieces):
        share = shares[6][index] if index < half else shares[7][index - half]
        place(index, share, start)
    roots.wait()
    for index in range(pieces):
        place(index, both_ref[index, :ROWS], rep * width)

    right_root = both_ref[:, ROWS:].reshape(order, width)
    rooted = []
    for part, copy in enumerate(blocks):
        copy.wait()
        lines = block_ref[part * (pieces // parts) : (part + 1) * (pieces // parts)]
        rooted.append(
            jnp.dot(
                lines.reshape(order // parts, order), right_root, preferred_element_type=F32
            ).astype(BF16)
        )
    rooted = jnp.concatenate(rooted, axis=0)
    precond = jnp.dot(left_ref[...], rooted, preferred_element_type=F32)
    out_ref[:, :ROWS, :] = precond.astype(BF16).reshape(pieces, rows, width)

    block = block_ref[...].reshape(order, order)
    columns = pl.multiple_of(rep * width, width)
    own_columns = block_ref[:, :, pl.ds(columns, width)].reshape(order, width)
    own_rows = block_ref[pl.ds(rep * (width // rows), width // rows)].reshape(width, order)
    left = lax.dot_general(
        own_rows, block, (((1,), (1,)), ((), ())), preferred_element_type=F32
    ).astype(BF16)
    for index in range(pieces):
        row, column = row_piece(index)
        for at, first in enumerate((column, column + width)):
            tile = left[row : row + TILE, first : first + width]
            base = ROWS + at * TILE
            out_ref[index, base : base + TILE] = tile
            own_ref[index, at * TILE : (at + 1) * TILE] = tile
    right = jnp.dot(own_columns.T, block, preferred_element_type=F32).T
    right = right.astype(BF16).reshape(pieces, rows, width)
    out_ref[:, 2 * ROWS : 3 * ROWS, :] = right
    own_ref[:, ROWS:, :] = right

    own = own_columns.astype(F32)
    lane = lax.broadcasted_iota(jnp.int32, (TILE, width), 1)
    total = jnp.zeros((TILE, width), F32)
    values = split_three(jnp.sum(precond * precond, keepdims=True))
    values += split_three(jnp.sum(own * own, keepdims=True))
    for index, value in enumerate(values):
        total = jnp.where(lane == index, value, total)
    out_ref[:, 3 * ROWS :, :] = jnp.broadcast_to(total.astype(BF16), (pieces, TILE, width))


def block_shares(rep, block, both, shares):
    pieces, _, order = block.shape
    vmem = pl.BlockSpec(memory_space=pltpu.VMEM)
    hbm = pl.BlockSpec(memory_space=pltpu.HBM)
    return pl.pallas_call(
        block_kernel,
        in_specs=[pl.BlockSpec(memory_space=pltpu.SMEM), hbm, hbm] + [vmem] * len(shares),
        out_specs=[vmem, vmem],
        out_shape=[
            jax.ShapeDtypeStruct((pieces, 3 * ROWS + TILE, LANES), BF16),
            jax.ShapeDtypeStruct((pieces, 2 * ROWS, LANES), BF16),
        ],
        scratch_shapes=[
            pltpu.VMEM(block.shape, BF16),
            pltpu.VMEM(both.shape, BF16),
            pltpu.VMEM((order, order), BF16),
            pltpu.SemaphoreType.DMA((5,)),
        ],
        compiler_params=params(20),
        cost_estimate=cost(8 * order * order * LANES, 6 * order * order),
        name="block_shares",
    )(rep, *in_hbm(block, both), *shares)


def named_kernel(arrived_ref, update_ref):
    count = arrived_ref.shape[0]
    line = lax.broadcasted_iota(jnp.int32, (ROWS, LANES), 0)
    sums = jnp.zeros((ROWS, LANES), F32)
    for index in range(count):
        update_ref[index] = arrived_ref[index, :ROWS, :]
        tail = arrived_ref[index, 3 * ROWS :, :].astype(F32)
        sums = jnp.where(line == index, jnp.concatenate([tail, tail], axis=0), sums)
    update_ref[count] = sums.astype(BF16)


def named(arrived):
    return pl.pallas_call(
        named_kernel,
        out_shape=jax.ShapeDtypeStruct((arrived.shape[0] + 1, ROWS, LANES), BF16),
        compiler_params=params(8),
        name="named",
    )(arrived)


def deal_kernel(plan_ref, arrived_ref, products_ref):
    spares = products_ref.shape[1] // (2 * ROWS)
    for owner in range(products_ref.shape[0]):
        for spare in range(spares):
            home = plan_ref[SPARE_HOME + owner * spares + spare]
            products_ref[owner, 2 * ROWS * spare : 2 * ROWS * (spare + 1)] = arrived_ref[
                home, ROWS : 3 * ROWS, :
            ]


def deal(plan, arrived, spares):
    shape = (arrived.shape[0], spares * 2 * ROWS, LANES)
    return pl.pallas_call(
        deal_kernel,
        in_specs=[
            pl.BlockSpec(memory_space=pltpu.SMEM),
            pl.BlockSpec(memory_space=pltpu.VMEM),
        ],
        out_shape=jax.ShapeDtypeStruct(shape, BF16),
        compiler_params=params(8),
        name="deal",
    )(plan, arrived)


def finish_kernel(rep_ref, plan_ref, *refs):
    shares, (out_hbm, out_ref, scale_ref, sems) = refs[:-4], refs[-4:]
    count, rows, order = out_ref.shape
    width = LANES
    half = shares[7].shape[0]
    replicas = order // width
    sums = shares[8][count - half].astype(F32)
    for share in shares[:7]:
        sums += share[count].astype(F32)
    lane = lax.broadcasted_iota(jnp.int32, (rows, width), 1)
    pre = jnp.sum(jnp.where(lane < 3, sums, 0.0), axis=1, keepdims=True)
    grad = jnp.sum(jnp.where((lane >= 3) & (lane < 6), sums, 0.0), axis=1, keepdims=True)
    scale = jnp.sqrt(grad) / jnp.sqrt(pre + epsilon)
    scale_ref[...] = jnp.broadcast_to(scale, (rows, width))

    def place(index, share, column):
        factor = scale_ref[pl.ds(index, 1), :]
        start = pl.multiple_of(column * width, width)
        out_ref[index, :, pl.ds(start, width)] = (share.astype(F32) * factor).astype(BF16)

    copies = []
    for index in range(count):
        for share, distance in zip(shares[:7], DISTANCES):
            place(index, share[index], lax.rem(rep_ref[0] - distance + replicas, replicas))
        far = lax.rem(rep_ref[0] + replicas // 2, replicas)
        share = shares[7][index] if index < half else shares[8][index - half]
        place(index, share, far)
        block = plan_ref[HOME_BLOCK + index]
        copies.append(pltpu.make_async_copy(out_ref.at[index], out_hbm.at[block], sems.at[index]))
        copies[-1].start()
    for copy in copies:
        copy.wait()


def finish(rep, plan, shares, count, rows, order):
    shape = (count, rows, order)
    return pl.pallas_call(
        finish_kernel,
        in_specs=[pl.BlockSpec(memory_space=pltpu.SMEM)] * 2
        + [pl.BlockSpec(memory_space=pltpu.VMEM)] * len(shares),
        out_specs=pl.BlockSpec(memory_space=pltpu.HBM),
        out_shape=jax.ShapeDtypeStruct(shape, BF16),
        scratch_shapes=[
            pltpu.VMEM(shape, BF16),
            pltpu.VMEM((count, LANES), F32),
            pltpu.SemaphoreType.DMA((count,)),
        ],
        compiler_params=params(12),
        name="finish",
    )(rep, plan, *shares)


def factor_kernel(
    plan_ref,
    place_ref,
    own_ref,
    products_ref,
    left_hbm,
    right_hbm,
    left_out,
    right_out,
    *scratch,
):
    left_ref, right_ref, left_new, right_new, held_ref, sems = scratch
    pieces = products_ref.shape[0]
    slots, order, width = right_ref.shape
    reads, writes = [], []
    for slot in range(slots):
        reads.append(
            (
                pltpu.make_async_copy(left_hbm.at[0, slot], left_ref.at[slot], sems.at[0, slot]),
                pltpu.make_async_copy(right_hbm.at[0, slot], right_ref.at[slot], sems.at[1, slot]),
            )
        )
        writes.append(
            (
                pltpu.make_async_copy(left_new.at[slot], left_out.at[0, slot], sems.at[2, slot]),
                pltpu.make_async_copy(right_new.at[slot], right_out.at[0, slot], sems.at[3, slot]),
            )
        )
        for copy in reads[slot]:
            copy.start()
    held_ref[0] = own_ref[...]
    for spare in range(slots - 1):
        held_ref[spare + 1] = products_ref[:, 2 * ROWS * spare : 2 * ROWS * (spare + 1)]
    which = jnp.int32(0)
    for slot in range(slots):
        named = plan_ref[SOURCE + place_ref[1] * slots + slot] >= 0
        weight = jnp.where(named, 1.0 - decay_rate, 0.0).astype(F32)
        for copy in reads[slot]:
            copy.wait()
        at_most = jnp.minimum(which, slots - 1)
        for index in range(pieces):
            row, column = row_piece(index)
            piece = held_ref[at_most, index].astype(F32)
            for part in range(2):
                at = (slot, pl.ds(row, TILE), pl.ds(column + part * width, width))
                product = piece[part * TILE : (part + 1) * TILE]
                left_new[at] = decay_rate * left_ref[at] + weight * product
            at = (slot, pl.ds(ROWS * index, ROWS))
            right_new[at] = decay_rate * right_ref[at] + weight * piece[ROWS:]
        for copy in writes[slot]:
            copy.start()
        which += named.astype(jnp.int32)
    for slot in range(slots):
        for copy in writes[slot]:
            copy.wait()


def factors(plan, place, own, products, left, right):
    slots, width, order = left.shape[1:]
    hbm = pl.BlockSpec(memory_space=pltpu.HBM)
    return pl.pallas_call(
        factor_kernel,
        in_specs=[
            pl.BlockSpec(memory_space=pltpu.SMEM),
            pl.BlockSpec(memory_space=pltpu.SMEM),
            pl.BlockSpec(memory_space=pltpu.VMEM),
            pl.BlockSpec(memory_space=pltpu.VMEM),
            hbm,
            hbm,
        ],
        out_specs=[hbm, hbm],
        out_shape=[
            jax.ShapeDtypeStruct(left.shape, F32),
            jax.ShapeDtypeStruct(right.shape, F32),
        ],
        scratch_shapes=[
            pltpu.VMEM((slots, width, order), F32),
            pltpu.VMEM((slots, order, width), F32),
            pltpu.VMEM((slots, width, order), F32),
            pltpu.VMEM((slots, order, width), F32),
            pltpu.VMEM((slots,) + own.shape, BF16),
            pltpu.SemaphoreType.DMA((4, slots)),
        ],
        compiler_params=params(16),
        cost_estimate=cost(2 * slots * order * order, 5 * slots * order * order),
        name="factors",
    )(plan, place, own, products, *in_hbm(left, right))


def ring_gather(share, axis, before_last=None):
    size = lax.axis_size(axis)
    half = share.shape[0] // 2

    def shift(value, by):
        return lax.ppermute(value, axis, [(i, (i + by) % size) for i in range(size)])

    down = [share, shift(share, -1)]
    up = [share, *anchor(shift(share, 1))]
    for _ in range(size // 2 - 2):
        down.append(shift(down[-1], -1))
        up.append(shift(up[-1], 1))
    if before_last is not None:
        up[-1], down[-1], before_last = lax.optimization_barrier((up[-1], down[-1], before_last))
    far_down = shift(down[-1][half:], -1)
    far_up = shift(up[-1][:half], 1)
    return up + down[1:] + [far_up, far_down], before_last


def anchor_kernel(*refs):
    del refs


def anchor(*arrays):
    hbm = pl.BlockSpec(memory_space=pl.ANY)
    return pl.pallas_call(
        anchor_kernel,
        in_specs=[hbm] * len(arrays),
        out_specs=[hbm] * len(arrays),
        out_shape=[jax.ShapeDtypeStruct(array.shape, array.dtype) for array in arrays],
        input_output_aliases={index: index for index in range(len(arrays))},
        compiler_params=params(4),
        cost_estimate=cost(1 << 38, 1 << 10),
        name="anchor",
    )(*arrays)


def exchange(value):
    return lax.all_to_all(value, "fsdp", split_axis=0, concat_axis=0, tiled=True)


def local(gradient, block_owner, block_slot, left_state, right_state, left_root, right_root):
    owners = lax.axis_size("fsdp")
    count, rows, order = gradient.shape
    slots = left_state.shape[1]
    rep = lax.axis_index("rep").astype(jnp.int32).reshape(1)
    place = jnp.concatenate([rep, lax.axis_index("fsdp").astype(jnp.int32).reshape(1)])
    plan = make_plan(block_owner, block_slot)

    spare = pack(place, block_owner, block_slot, left_root[0], right_root[0], owners)
    kept = keep(place, plan, left_root[0], right_root[0], owners)
    roots = exchange(route(plan, exchange(spare)))
    left, both = pick(place, plan, kept, roots)
    packed, left = lax.optimization_barrier((gather(plan, gradient), left))
    left_shares, _ = ring_gather(left, "rep")
    outgoing, own = block_shares(rep, exchange(packed), both, left_shares[1:])

    arrived = exchange(outgoing)
    products = exchange(deal(plan, arrived, slots - 1))
    outputs = factors(plan, place, own, products, left_state, right_state)
    shares, outputs = ring_gather(named(arrived), "rep", outputs)
    left_factor, right_factor = outputs
    update = finish(rep, plan, shares, count, rows, order)
    return (update, left_factor, right_factor)


def solution(mesh):
    in_specs = (
        P(None, "fsdp", None),
        P(),
        P(),
        P("fsdp", None, "rep", None),
        P("fsdp", None, None, "rep"),
        P("fsdp", None, "rep", None),
        P("fsdp", None, None, "rep"),
    )
    out_specs = (P(None, "fsdp", None), P("fsdp", None, "rep", None), P("fsdp", None, None, "rep"))
    return jax.shard_map(local, mesh=mesh, in_specs=in_specs, out_specs=out_specs, check_vma=False)
```

```python
import jax
import jax.numpy as jnp
from jax import lax
from jax.experimental import pallas as pl
from jax.experimental.pallas import tpu as pltpu
from jax.sharding import PartitionSpec as P

decay_rate = 0.95
epsilon = 1e-06

F32 = jnp.float32
BF16 = jnp.bfloat16
ROWS = 32
TILE = 16
LANES = 128
DISTANCES = (0, 1, 2, 3, -1, -2, -3, 4)


def params(mebibytes):
    return pltpu.CompilerParams(vmem_limit_bytes=mebibytes * 1024 * 1024)


def in_hbm(*arrays):
    return [pltpu.with_memory_space_constraint(array, pltpu.HBM) for array in arrays]


def cost(flops, accessed):
    return pl.CostEstimate(flops=flops, bytes_accessed=accessed, transcendentals=0)


def whole(shape):
    return pl.BlockSpec(shape, lambda *_: (0,) * len(shape))


def row_piece(index):
    per_line = 1024 // (2 * LANES)
    return TILE * (index // per_line), 2 * LANES * (index % per_line)


def split_three(value):
    high = value.astype(BF16).astype(F32)
    rest = value - high
    middle = rest.astype(BF16).astype(F32)
    return high, middle, (rest - middle).astype(BF16).astype(F32)


SOURCE = 0
HOME_BLOCK = 96
HOME_ORIGIN = 128
SPARE_HOME = 160
PLAN = 256


def plan_kernel(owner_ref, slot_ref, plan_ref, list_ref):
    owners = HOME_ORIGIN - HOME_BLOCK
    slots = (HOME_BLOCK - SOURCE) // owners

    def clear(index, carry):
        plan_ref[SOURCE + index] = -1
        return carry

    def clear_spare(index, carry):
        plan_ref[SPARE_HOME + index] = 0
        return carry

    def enter(index, carry):
        plan_ref[SOURCE + owner_ref[index] * slots + slot_ref[index]] = index
        return carry

    def walk(owner, carry):
        spare, idle = carry
        count = 0
        for slot in range(slots):
            block = plan_ref[SOURCE + owner * slots + slot]
            named = block >= 0

            @pl.when(named & (count == 0))
            def _():
                plan_ref[HOME_BLOCK + owner] = block
                plan_ref[HOME_ORIGIN + owner] = -1

            @pl.when(named & (count > 0))
            def _():
                list_ref[0, spare] = block
                list_ref[1, spare] = owner * 2 + count - 1

            spare += (named & (count > 0)).astype(jnp.int32)
            count += named.astype(jnp.int32)

        @pl.when(count == 0)
        def _():
            list_ref[2, idle] = owner

        return spare, idle + (count == 0).astype(jnp.int32)

    def assign(index, carry):
        home = list_ref[2, index]
        origin = list_ref[1, index]
        plan_ref[HOME_BLOCK + home] = list_ref[0, index]
        plan_ref[HOME_ORIGIN + home] = origin
        plan_ref[SPARE_HOME + origin] = home
        return carry

    zero = jnp.int32(0)
    lax.fori_loop(0, owners * slots, clear, zero)
    lax.fori_loop(0, 2 * owners, clear_spare, zero)
    lax.fori_loop(0, owner_ref.shape[0], enter, zero)
    _, idle = lax.fori_loop(0, owners, walk, (zero, zero))
    lax.fori_loop(0, idle, assign, zero)


def make_plan(owner, slot):
    smem = pl.BlockSpec(memory_space=pltpu.SMEM)
    return pl.pallas_call(
        plan_kernel,
        in_specs=[smem, smem],
        out_specs=smem,
        out_shape=jax.ShapeDtypeStruct((PLAN,), jnp.int32),
        scratch_shapes=[pltpu.SMEM((3, 32), jnp.int32)],
        compiler_params=params(4),
        name="make_plan",
    )(owner, slot)


def cut(left_ref, right_ref, slot, out_ref, base):
    for index in range(out_ref.shape[0]):
        row, column = row_piece(index)
        rows = pl.ds(row, TILE)
        out_ref[index, base : base + TILE] = left_ref[slot, rows, column : column + LANES]
        out_ref[index, base + TILE : base + ROWS] = left_ref[
            slot, rows, column + LANES : column + 2 * LANES
        ]
        out_ref[index, base + ROWS : base + 2 * ROWS] = right_ref[
            slot, ROWS * index : ROWS * (index + 1)
        ]


def pack_kernel(
    place_ref, owner_hbm, slot_hbm, left_hbm, right_hbm, spare_hbm, *scratch
):
    owner_ref, slot_ref, left_ref, right_ref, spare_ref, sems = scratch
    spares = left_ref.shape[0]
    roots = []
    for spare in range(spares):
        pair = (
            pltpu.make_async_copy(left_hbm.at[spare + 1], left_ref.at[spare], sems.at[0, spare]),
            pltpu.make_async_copy(right_hbm.at[spare + 1], right_ref.at[spare], sems.at[1, spare]),
        )
        roots.append(pair)
    names = (
        pltpu.make_async_copy(owner_hbm, owner_ref, sems.at[2, 0]),
        pltpu.make_async_copy(slot_hbm, slot_ref, sems.at[2, 1]),
    )
    for copy in names + roots[1] + roots[0]:
        copy.start()
    for copy in names:
        copy.wait()

    def look(index, found):
        own = owner_ref[index] == place_ref[1]
        return found + (own & (slot_ref[index] < spares)).astype(jnp.int32)

    found = lax.fori_loop(0, owner_ref.shape[0], look, jnp.int32(0), unroll=4)
    second = jnp.where(found == spares, 0, 1)
    for copy in roots[1]:
        copy.wait()
    writes = []
    for spare in (1, 0):
        if spare == 0:
            for copy in roots[0]:
                copy.wait()
        cut(left_ref, right_ref, 1 if spare else second, spare_ref, 2 * ROWS * spare)
        part = (slice(None), pl.ds(2 * ROWS * spare, 2 * ROWS))
        copy = pltpu.make_async_copy(spare_ref.at[part], spare_hbm.at[part], sems.at[3, spare])
        copy.start()
        writes.append(copy)
    for copy in writes:
        copy.wait()


def pack(place, owner, slot, left, right, pieces):
    hbm = pl.BlockSpec(memory_space=pltpu.HBM)
    spares = left.shape[0] - 1
    shape = (pieces, spares * 2 * ROWS, LANES)
    return pl.pallas_call(
        pack_kernel,
        in_specs=[pl.BlockSpec(memory_space=pltpu.SMEM)] + [hbm] * 4,
        out_specs=hbm,
        out_shape=pltpu.HBM(shape, BF16),
        scratch_shapes=[
            pltpu.SMEM(owner.shape, jnp.int32),
            pltpu.SMEM(slot.shape, jnp.int32),
            pltpu.VMEM((spares,) + left.shape[1:], BF16),
            pltpu.VMEM((spares,) + right.shape[1:], BF16),
            pltpu.VMEM(shape, BF16),
            pltpu.SemaphoreType.DMA((4, 2)),
        ],
        compiler_params=params(8),
        name="pack",
    )(place, *in_hbm(owner, slot, left, right))


def keep_kernel(place_ref, plan_ref, left_hbm, right_hbm, kept_ref, left_ref, right_ref, sems):
    slots = left_hbm.shape[0]
    first = jnp.int32(slots - 1)
    for slot in reversed(range(slots - 1)):
        first = jnp.where(plan_ref[SOURCE + place_ref[1] * slots + slot] >= 0, slot, first)
    copies = (
        pltpu.make_async_copy(left_hbm.at[first], left_ref.at[0], sems.at[0]),
        pltpu.make_async_copy(right_hbm.at[first], right_ref.at[0], sems.at[1]),
    )
    for copy in copies:
        copy.start()
    for copy in copies:
        copy.wait()
    cut(left_ref, right_ref, 0, kept_ref, 0)


def keep(place, plan, left, right, pieces):
    smem = pl.BlockSpec(memory_space=pltpu.SMEM)
    hbm = pl.BlockSpec(memory_space=pltpu.HBM)
    return pl.pallas_call(
        keep_kernel,
        in_specs=[smem, smem, hbm, hbm],
        out_specs=pl.BlockSpec(memory_space=pltpu.VMEM),
        out_shape=jax.ShapeDtypeStruct((pieces, 2 * ROWS, LANES), BF16),
        scratch_shapes=[
            pltpu.VMEM((1,) + left.shape[1:], BF16),
            pltpu.VMEM((1,) + right.shape[1:], BF16),
            pltpu.SemaphoreType.DMA((2,)),
        ],
        compiler_params=params(8),
        name="keep",
    )(place, plan, *in_hbm(left, right))


def route_kernel(plan_ref, arrived_ref, out_hbm, sems):
    copies = []
    for home in range(out_hbm.shape[0]):
        origin = jnp.maximum(plan_ref[HOME_ORIGIN + home], 0)
        start = pl.multiple_of(lax.rem(origin, 2) * (2 * ROWS), 2 * ROWS)
        source = arrived_ref.at[lax.div(origin, 2), pl.ds(start, 2 * ROWS)]
        copies.append(pltpu.make_async_copy(source, out_hbm.at[home], sems.at[home]))
        copies[-1].start()
    for copy in copies:
        copy.wait()


def route(plan, arrived):
    homes = arrived.shape[0]
    return pl.pallas_call(
        route_kernel,
        in_specs=[
            pl.BlockSpec(memory_space=pltpu.SMEM),
            pl.BlockSpec(memory_space=pltpu.VMEM),
        ],
        out_specs=pl.BlockSpec(memory_space=pltpu.HBM),
        out_shape=pltpu.HBM((homes, 2 * ROWS, LANES), BF16),
        scratch_shapes=[pltpu.SemaphoreType.DMA((homes,))],
        compiler_params=params(8),
        name="route",
    )(plan, arrived)


def pick_kernel(place_ref, plan_ref, kept_ref, roots_ref, left_ref, both_hbm, sem):
    own = plan_ref[HOME_ORIGIN + place_ref[1]] < 0

    def take(source_ref):
        copy = pltpu.make_async_copy(source_ref, both_hbm, sem)
        copy.start()
        left_ref[...] = source_ref[:, :ROWS]
        copy.wait()

    @pl.when(own)
    def _():
        take(kept_ref)

    @pl.when(jnp.logical_not(own))
    def _():
        take(roots_ref)


def pick(place, plan, kept, roots):
    smem = pl.BlockSpec(memory_space=pltpu.SMEM)
    vmem = pl.BlockSpec(memory_space=pltpu.VMEM)
    return pl.pallas_call(
        pick_kernel,
        in_specs=[smem, smem, vmem, vmem],
        out_specs=[vmem, pl.BlockSpec(memory_space=pltpu.HBM)],
        out_shape=[
            jax.ShapeDtypeStruct((kept.shape[0], ROWS, LANES), BF16),
            pltpu.HBM(kept.shape, BF16),
        ],
        scratch_shapes=[pltpu.SemaphoreType.DMA],
        compiler_params=params(8),
        name="pick",
    )(place, plan, kept, roots)


def gather_kernel(plan_ref, gradient_ref, out_ref):
    for home in range(out_ref.shape[0]):
        out_ref[home] = gradient_ref[plan_ref[HOME_BLOCK + home]]


def gather(plan, gradient):
    return pl.pallas_call(
        gather_kernel,
        in_specs=[
            pl.BlockSpec(memory_space=pltpu.SMEM),
            pl.BlockSpec(memory_space=pltpu.VMEM),
        ],
        out_shape=jax.ShapeDtypeStruct(gradient.shape, BF16),
        compiler_params=params(8),
        name="gather",
    )(plan, gradient)


def block_kernel(rep_ref, block_hbm, both_hbm, *refs):
    shares, (out_ref, own_ref, block_ref, both_ref, left_ref, sems) = refs[:-6], refs[-6:]
    pieces, rows, order = block_ref.shape
    width = LANES
    replicas = order // width
    rep = rep_ref[0]
    roots = pltpu.make_async_copy(both_hbm, both_ref, sems.at[0])
    roots.start()
    parts = 4
    blocks = []
    for part in range(parts):
        lines = pl.ds(part * (pieces // parts), pieces // parts)
        copy = pltpu.make_async_copy(
            block_hbm.at[lines], block_ref.at[lines], sems.at[1 + part]
        )
        copy.start()
        blocks.append(copy)

    def place(index, share, start):
        row, column = row_piece(index)
        lines = pl.ds(pl.multiple_of(start + row, TILE), TILE)
        left_ref[lines, column : column + width] = share[:TILE]
        left_ref[lines, column + width : column + 2 * width] = share[TILE:]

    for share, distance in zip(shares, DISTANCES[1:]):
        start = lax.rem(rep - distance + replicas, replicas) * width
        for index in range(pieces):
            place(index, share[index], start)
    roots.wait()
    for index in range(pieces):
        place(index, both_ref[index, :ROWS], rep * width)

    right_root = both_ref[:, ROWS:].reshape(order, width)
    rooted = []
    for part, copy in enumerate(blocks):
        copy.wait()
        lines = block_ref[part * (pieces // parts) : (part + 1) * (pieces // parts)]
        rooted.append(
            jnp.dot(
                lines.reshape(order // parts, order), right_root, preferred_element_type=F32
            ).astype(BF16)
        )
    rooted = jnp.concatenate(rooted, axis=0)
    precond = jnp.dot(left_ref[...], rooted, preferred_element_type=F32)
    out_ref[:, :ROWS, :] = precond.astype(BF16).reshape(pieces, rows, width)

    block = block_ref[...].reshape(order, order)
    columns = pl.multiple_of(rep * width, width)
    own_columns = block_ref[:, :, pl.ds(columns, width)].reshape(order, width)
    own_rows = block_ref[pl.ds(rep * (width // rows), width // rows)].reshape(width, order)
    left = lax.dot_general(
        own_rows, block, (((1,), (1,)), ((), ())), preferred_element_type=F32
    ).astype(BF16)
    for index in range(pieces):
        row, column = row_piece(index)
        for at, first in enumerate((column, column + width)):
            tile = left[row : row + TILE, first : first + width]
            base = ROWS + at * TILE
            out_ref[index, base : base + TILE] = tile
            own_ref[index, at * TILE : (at + 1) * TILE] = tile
    right = jnp.dot(own_columns.T, block, preferred_element_type=F32).T
    right = right.astype(BF16).reshape(pieces, rows, width)
    out_ref[:, 2 * ROWS : 3 * ROWS, :] = right
    own_ref[:, ROWS:, :] = right

    own = own_columns.astype(F32)
    lane = lax.broadcasted_iota(jnp.int32, (TILE, width), 1)
    total = jnp.zeros((TILE, width), F32)
    values = split_three(jnp.sum(precond * precond, keepdims=True))
    values += split_three(jnp.sum(own * own, keepdims=True))
    for index, value in enumerate(values):
        total = jnp.where(lane == index, value, total)
    out_ref[:, 3 * ROWS :, :] = jnp.broadcast_to(total.astype(BF16), (pieces, TILE, width))


def block_shares(rep, block, both, shares):
    pieces, _, order = block.shape
    vmem = pl.BlockSpec(memory_space=pltpu.VMEM)
    hbm = pl.BlockSpec(memory_space=pltpu.HBM)
    return pl.pallas_call(
        block_kernel,
        in_specs=[pl.BlockSpec(memory_space=pltpu.SMEM), hbm, hbm] + [vmem] * len(shares),
        out_specs=[vmem, vmem],
        out_shape=[
            jax.ShapeDtypeStruct((pieces, 3 * ROWS + TILE, LANES), BF16),
            jax.ShapeDtypeStruct((pieces, 2 * ROWS, LANES), BF16),
        ],
        scratch_shapes=[
            pltpu.VMEM(block.shape, BF16),
            pltpu.VMEM(both.shape, BF16),
            pltpu.VMEM((order, order), BF16),
            pltpu.SemaphoreType.DMA((5,)),
        ],
        compiler_params=params(20),
        cost_estimate=cost(8 * order * order * LANES, 6 * order * order),
        name="block_shares",
    )(rep, *in_hbm(block, both), *shares)


def named_kernel(arrived_ref, update_ref):
    count = arrived_ref.shape[0]
    line = lax.broadcasted_iota(jnp.int32, (ROWS, LANES), 0)
    sums = jnp.zeros((ROWS, LANES), F32)
    for index in range(count):
        update_ref[index] = arrived_ref[index, :ROWS, :]
        tail = arrived_ref[index, 3 * ROWS :, :].astype(F32)
        sums = jnp.where(line == index, jnp.concatenate([tail, tail], axis=0), sums)
    update_ref[count] = sums.astype(BF16)


def named(arrived):
    return pl.pallas_call(
        named_kernel,
        out_shape=jax.ShapeDtypeStruct((arrived.shape[0] + 1, ROWS, LANES), BF16),
        compiler_params=params(8),
        name="named",
    )(arrived)


def deal_kernel(plan_ref, arrived_ref, products_ref):
    spares = products_ref.shape[1] // (2 * ROWS)
    for owner in range(products_ref.shape[0]):
        for spare in range(spares):
            home = plan_ref[SPARE_HOME + owner * spares + spare]
            products_ref[owner, 2 * ROWS * spare : 2 * ROWS * (spare + 1)] = arrived_ref[
                home, ROWS : 3 * ROWS, :
            ]


def deal(plan, arrived, spares):
    shape = (arrived.shape[0], spares * 2 * ROWS, LANES)
    return pl.pallas_call(
        deal_kernel,
        in_specs=[
            pl.BlockSpec(memory_space=pltpu.SMEM),
            pl.BlockSpec(memory_space=pltpu.VMEM),
        ],
        out_shape=jax.ShapeDtypeStruct(shape, BF16),
        compiler_params=params(8),
        name="deal",
    )(plan, arrived)


def finish_kernel(rep_ref, plan_ref, *refs):
    shares, (out_hbm, out_ref, scale_ref, sems) = refs[:-4], refs[-4:]
    count, rows, order = out_ref.shape
    width = LANES
    replicas = order // width
    sums = shares[0][count].astype(F32)
    for share in shares[1:]:
        sums += share[count].astype(F32)
    lane = lax.broadcasted_iota(jnp.int32, (rows, width), 1)
    pre = jnp.sum(jnp.where(lane < 3, sums, 0.0), axis=1, keepdims=True)
    grad = jnp.sum(jnp.where((lane >= 3) & (lane < 6), sums, 0.0), axis=1, keepdims=True)
    scale = jnp.sqrt(grad) / jnp.sqrt(pre + epsilon)
    scale_ref[...] = jnp.broadcast_to(scale, (rows, width))

    def place(index, share, column):
        factor = scale_ref[pl.ds(index, 1), :]
        start = pl.multiple_of(column * width, width)
        out_ref[index, :, pl.ds(start, width)] = (share.astype(F32) * factor).astype(BF16)

    copies = []
    for index in range(count):
        for share, distance in zip(shares, DISTANCES):
            place(index, share[index], lax.rem(rep_ref[0] - distance + replicas, replicas))
        block = plan_ref[HOME_BLOCK + index]
        copies.append(pltpu.make_async_copy(out_ref.at[index], out_hbm.at[block], sems.at[index]))
        copies[-1].start()
    for copy in copies:
        copy.wait()


def finish(rep, plan, shares, count, rows, order):
    shape = (count, rows, order)
    return pl.pallas_call(
        finish_kernel,
        in_specs=[pl.BlockSpec(memory_space=pltpu.SMEM)] * 2
        + [pl.BlockSpec(memory_space=pltpu.VMEM)] * len(shares),
        out_specs=pl.BlockSpec(memory_space=pltpu.HBM),
        out_shape=jax.ShapeDtypeStruct(shape, BF16),
        scratch_shapes=[
            pltpu.VMEM(shape, BF16),
            pltpu.VMEM((count, LANES), F32),
            pltpu.SemaphoreType.DMA((count,)),
        ],
        compiler_params=params(12),
        name="finish",
    )(rep, plan, *shares)


def factor_kernel(
    plan_ref,
    place_ref,
    own_ref,
    products_ref,
    left_hbm,
    right_hbm,
    left_out,
    right_out,
    *scratch,
):
    left_ref, right_ref, left_new, right_new, held_ref, sems = scratch
    pieces = products_ref.shape[0]
    slots, order, width = right_ref.shape
    reads, writes = [], []
    for slot in range(slots):
        reads.append(
            (
                pltpu.make_async_copy(left_hbm.at[0, slot], left_ref.at[slot], sems.at[0, slot]),
                pltpu.make_async_copy(right_hbm.at[0, slot], right_ref.at[slot], sems.at[1, slot]),
            )
        )
        writes.append(
            (
                pltpu.make_async_copy(left_new.at[slot], left_out.at[0, slot], sems.at[2, slot]),
                pltpu.make_async_copy(right_new.at[slot], right_out.at[0, slot], sems.at[3, slot]),
            )
        )
        for copy in reads[slot]:
            copy.start()
    held_ref[0] = own_ref[...]
    for spare in range(slots - 1):
        held_ref[spare + 1] = products_ref[:, 2 * ROWS * spare : 2 * ROWS * (spare + 1)]
    which = jnp.int32(0)
    for slot in range(slots):
        named = plan_ref[SOURCE + place_ref[1] * slots + slot] >= 0
        weight = jnp.where(named, 1.0 - decay_rate, 0.0).astype(F32)
        for copy in reads[slot]:
            copy.wait()
        at_most = jnp.minimum(which, slots - 1)
        for index in range(pieces):
            row, column = row_piece(index)
            piece = held_ref[at_most, index].astype(F32)
            for part in range(2):
                at = (slot, pl.ds(row, TILE), pl.ds(column + part * width, width))
                product = piece[part * TILE : (part + 1) * TILE]
                left_new[at] = decay_rate * left_ref[at] + weight * product
            at = (slot, pl.ds(ROWS * index, ROWS))
            right_new[at] = decay_rate * right_ref[at] + weight * piece[ROWS:]
        for copy in writes[slot]:
            copy.start()
        which += named.astype(jnp.int32)
    for slot in range(slots):
        for copy in writes[slot]:
            copy.wait()


def factors(plan, place, own, products, left, right):
    slots, width, order = left.shape[1:]
    hbm = pl.BlockSpec(memory_space=pltpu.HBM)
    return pl.pallas_call(
        factor_kernel,
        in_specs=[
            pl.BlockSpec(memory_space=pltpu.SMEM),
            pl.BlockSpec(memory_space=pltpu.SMEM),
            pl.BlockSpec(memory_space=pltpu.VMEM),
            pl.BlockSpec(memory_space=pltpu.VMEM),
            hbm,
            hbm,
        ],
        out_specs=[hbm, hbm],
        out_shape=[
            jax.ShapeDtypeStruct(left.shape, F32),
            jax.ShapeDtypeStruct(right.shape, F32),
        ],
        scratch_shapes=[
            pltpu.VMEM((slots, width, order), F32),
            pltpu.VMEM((slots, order, width), F32),
            pltpu.VMEM((slots, width, order), F32),
            pltpu.VMEM((slots, order, width), F32),
            pltpu.VMEM((slots,) + own.shape, BF16),
            pltpu.SemaphoreType.DMA((4, slots)),
        ],
        compiler_params=params(16),
        cost_estimate=cost(2 * slots * order * order, 5 * slots * order * order),
        name="factors",
    )(plan, place, own, products, *in_hbm(left, right))


def ring_gather(share):
    size = lax.axis_size("rep")
    owners = lax.axis_size("fsdp")

    def shift(value, by):
        return lax.ppermute(value, "rep", [(i, (i + by) % size) for i in range(size)])

    down = [share, shift(share, -1)]
    up = [share, *anchor(shift(share, 1))]
    for _ in range(size // 2 - 2):
        down.append(shift(down[-1], -1))
        up.append(shift(up[-1], 1))
    even = lax.axis_index("fsdp") % 2 == 0
    passed = lax.select(even, up[1], down[1])
    pairs = [
        (owner * size + i, owner * size + (i + (-3 if owner % 2 else 3)) % size)
        for owner in range(owners)
        for i in range(size)
    ]
    return up + down[1:] + [lax.ppermute(passed, ("fsdp", "rep"), pairs)]


def anchor_kernel(*refs):
    del refs


def anchor(*arrays):
    hbm = pl.BlockSpec(memory_space=pl.ANY)
    return pl.pallas_call(
        anchor_kernel,
        in_specs=[hbm] * len(arrays),
        out_specs=[hbm] * len(arrays),
        out_shape=[jax.ShapeDtypeStruct(array.shape, array.dtype) for array in arrays],
        input_output_aliases={index: index for index in range(len(arrays))},
        compiler_params=params(4),
        cost_estimate=cost(1 << 38, 1 << 10),
        name="anchor",
    )(*arrays)


def exchange(value):
    return lax.all_to_all(value, "fsdp", split_axis=0, concat_axis=0, tiled=True)


def local(gradient, block_owner, block_slot, left_state, right_state, left_root, right_root):
    owners = lax.axis_size("fsdp")
    count, rows, order = gradient.shape
    slots = left_state.shape[1]
    rep = lax.axis_index("rep").astype(jnp.int32).reshape(1)
    place = jnp.concatenate([rep, lax.axis_index("fsdp").astype(jnp.int32).reshape(1)])
    plan = make_plan(block_owner, block_slot)

    spare = pack(place, block_owner, block_slot, left_root[0], right_root[0], owners)
    kept = keep(place, plan, left_root[0], right_root[0], owners)
    roots = exchange(route(plan, exchange(spare)))
    left, both = pick(place, plan, kept, roots)
    packed, left = lax.optimization_barrier((gather(plan, gradient), left))
    left_shares = ring_gather(left)
    outgoing, own = block_shares(rep, exchange(packed), both, left_shares[1:])

    arrived = exchange(outgoing)
    products = exchange(deal(plan, arrived, slots - 1))
    left_factor, right_factor = factors(plan, place, own, products, left_state, right_state)
    shares = ring_gather(named(arrived))
    shares, left_factor, right_factor = lax.optimization_barrier(
        (shares, left_factor, right_factor)
    )
    update = finish(rep, plan, shares, count, rows, order)
    return (update, left_factor, right_factor)


def solution(mesh):
    in_specs = (
        P(None, "fsdp", None),
        P(),
        P(),
        P("fsdp", None, "rep", None),
        P("fsdp", None, None, "rep"),
        P("fsdp", None, "rep", None),
        P("fsdp", None, None, "rep"),
    )
    out_specs = (P(None, "fsdp", None), P("fsdp", None, "rep", None), P("fsdp", None, None, "rep"))
    return jax.shard_map(local, mesh=mesh, in_specs=in_specs, out_specs=out_specs, check_vma=False)
```

```python
import jax
import jax.numpy as jnp
from jax import lax
from jax.experimental import pallas as pl
from jax.experimental.pallas import tpu as pltpu
from jax.sharding import PartitionSpec as P

decay_rate = 0.95
epsilon = 1e-06

F32 = jnp.float32
BF16 = jnp.bfloat16
ROWS = 32
TILE = 16
LANES = 128
DISTANCES = (0, 1, 2, 3, -1, -2, -3, 4)


def params(mebibytes):
    return pltpu.CompilerParams(vmem_limit_bytes=mebibytes * 1024 * 1024)


def in_hbm(*arrays):
    return [pltpu.with_memory_space_constraint(array, pltpu.HBM) for array in arrays]


def cost(flops, accessed):
    return pl.CostEstimate(flops=flops, bytes_accessed=accessed, transcendentals=0)


def whole(shape):
    return pl.BlockSpec(shape, lambda *_: (0,) * len(shape))


def row_piece(index):
    per_line = 1024 // (2 * LANES)
    return TILE * (index // per_line), 2 * LANES * (index % per_line)


def split_three(value):
    high = value.astype(BF16).astype(F32)
    rest = value - high
    middle = rest.astype(BF16).astype(F32)
    return high, middle, (rest - middle).astype(BF16).astype(F32)


SOURCE = 0
HOME_BLOCK = 96
HOME_ORIGIN = 128
SPARE_HOME = 160
PLAN = 256


def plan_kernel(owner_ref, slot_ref, plan_ref, list_ref):
    owners = HOME_ORIGIN - HOME_BLOCK
    slots = (HOME_BLOCK - SOURCE) // owners

    def clear(index, carry):
        plan_ref[SOURCE + index] = -1
        return carry

    def clear_spare(index, carry):
        plan_ref[SPARE_HOME + index] = 0
        return carry

    def enter(index, carry):
        plan_ref[SOURCE + owner_ref[index] * slots + slot_ref[index]] = index
        return carry

    def walk(owner, carry):
        spare, idle = carry
        count = 0
        for slot in range(slots):
            block = plan_ref[SOURCE + owner * slots + slot]
            named = block >= 0

            @pl.when(named & (count == 0))
            def _():
                plan_ref[HOME_BLOCK + owner] = block
                plan_ref[HOME_ORIGIN + owner] = -1

            @pl.when(named & (count > 0))
            def _():
                list_ref[0, spare] = block
                list_ref[1, spare] = owner * 2 + slot - 1

            spare += (named & (count > 0)).astype(jnp.int32)
            count += named.astype(jnp.int32)

        @pl.when(count == 0)
        def _():
            list_ref[2, idle] = owner

        return spare, idle + (count == 0).astype(jnp.int32)

    def assign(index, carry):
        home = list_ref[2, index]
        origin = list_ref[1, index]
        plan_ref[HOME_BLOCK + home] = list_ref[0, index]
        plan_ref[HOME_ORIGIN + home] = origin
        plan_ref[SPARE_HOME + origin] = home
        return carry

    zero = jnp.int32(0)
    lax.fori_loop(0, owners * slots, clear, zero)
    lax.fori_loop(0, 2 * owners, clear_spare, zero)
    lax.fori_loop(0, owner_ref.shape[0], enter, zero)
    _, idle = lax.fori_loop(0, owners, walk, (zero, zero))
    lax.fori_loop(0, idle, assign, zero)


def make_plan(owner, slot):
    smem = pl.BlockSpec(memory_space=pltpu.SMEM)
    return pl.pallas_call(
        plan_kernel,
        in_specs=[smem, smem],
        out_specs=smem,
        out_shape=jax.ShapeDtypeStruct((PLAN,), jnp.int32),
        scratch_shapes=[pltpu.SMEM((3, 32), jnp.int32)],
        compiler_params=params(4),
        name="make_plan",
    )(owner, slot)


def cut(left_ref, right_ref, slot, out_ref, base):
    for index in range(out_ref.shape[0]):
        row, column = row_piece(index)
        rows = pl.ds(row, TILE)
        out_ref[index, base : base + TILE] = left_ref[slot, rows, column : column + LANES]
        out_ref[index, base + TILE : base + ROWS] = left_ref[
            slot, rows, column + LANES : column + 2 * LANES
        ]
        out_ref[index, base + ROWS : base + 2 * ROWS] = right_ref[
            slot, ROWS * index : ROWS * (index + 1)
        ]


def pack_kernel(left_hbm, right_hbm, spare_hbm, left_ref, right_ref, spare_ref, sems):
    reads, writes = [], []
    for spare in range(left_ref.shape[0]):
        pair = (
            pltpu.make_async_copy(left_hbm.at[spare + 1], left_ref.at[spare], sems.at[0, spare]),
            pltpu.make_async_copy(right_hbm.at[spare + 1], right_ref.at[spare], sems.at[1, spare]),
        )
        for copy in pair:
            copy.start()
        reads.append(pair)
    for spare, pair in enumerate(reads):
        for copy in pair:
            copy.wait()
        cut(left_ref, right_ref, spare, spare_ref, 2 * ROWS * spare)
        part = (slice(None), pl.ds(2 * ROWS * spare, 2 * ROWS))
        copy = pltpu.make_async_copy(spare_ref.at[part], spare_hbm.at[part], sems.at[2, spare])
        copy.start()
        writes.append(copy)
    for copy in writes:
        copy.wait()


def pack(left, right, pieces):
    hbm = pl.BlockSpec(memory_space=pltpu.HBM)
    spares = left.shape[0] - 1
    shape = (pieces, spares * 2 * ROWS, LANES)
    return pl.pallas_call(
        pack_kernel,
        in_specs=[hbm, hbm],
        out_specs=hbm,
        out_shape=pltpu.HBM(shape, BF16),
        scratch_shapes=[
            pltpu.VMEM((spares,) + left.shape[1:], BF16),
            pltpu.VMEM((spares,) + right.shape[1:], BF16),
            pltpu.VMEM(shape, BF16),
            pltpu.SemaphoreType.DMA((3, spares)),
        ],
        compiler_params=params(8),
        name="pack",
    )(*in_hbm(left, right))


def keep_kernel(place_ref, plan_ref, left_hbm, right_hbm, kept_ref, left_ref, right_ref, sems):
    slots = left_hbm.shape[0]
    first = jnp.int32(slots - 1)
    for slot in reversed(range(slots - 1)):
        first = jnp.where(plan_ref[SOURCE + place_ref[1] * slots + slot] >= 0, slot, first)
    copies = (
        pltpu.make_async_copy(left_hbm.at[first], left_ref.at[0], sems.at[0]),
        pltpu.make_async_copy(right_hbm.at[first], right_ref.at[0], sems.at[1]),
    )
    for copy in copies:
        copy.start()
    for copy in copies:
        copy.wait()
    cut(left_ref, right_ref, 0, kept_ref, 0)


def keep(place, plan, left, right, pieces):
    smem = pl.BlockSpec(memory_space=pltpu.SMEM)
    hbm = pl.BlockSpec(memory_space=pltpu.HBM)
    return pl.pallas_call(
        keep_kernel,
        in_specs=[smem, smem, hbm, hbm],
        out_specs=pl.BlockSpec(memory_space=pltpu.VMEM),
        out_shape=jax.ShapeDtypeStruct((pieces, 2 * ROWS, LANES), BF16),
        scratch_shapes=[
            pltpu.VMEM((1,) + left.shape[1:], BF16),
            pltpu.VMEM((1,) + right.shape[1:], BF16),
            pltpu.SemaphoreType.DMA((2,)),
        ],
        compiler_params=params(8),
        name="keep",
    )(place, plan, *in_hbm(left, right))


def route_kernel(plan_ref, arrived_ref, out_hbm, sems):
    copies = []
    for home in range(out_hbm.shape[0]):
        origin = jnp.maximum(plan_ref[HOME_ORIGIN + home], 0)
        start = pl.multiple_of(lax.rem(origin, 2) * (2 * ROWS), 2 * ROWS)
        source = arrived_ref.at[lax.div(origin, 2), pl.ds(start, 2 * ROWS)]
        copies.append(pltpu.make_async_copy(source, out_hbm.at[home], sems.at[home]))
        copies[-1].start()
    for copy in copies:
        copy.wait()


def route(plan, arrived):
    homes = arrived.shape[0]
    return pl.pallas_call(
        route_kernel,
        in_specs=[
            pl.BlockSpec(memory_space=pltpu.SMEM),
            pl.BlockSpec(memory_space=pltpu.VMEM),
        ],
        out_specs=pl.BlockSpec(memory_space=pltpu.HBM),
        out_shape=pltpu.HBM((homes, 2 * ROWS, LANES), BF16),
        scratch_shapes=[pltpu.SemaphoreType.DMA((homes,))],
        compiler_params=params(8),
        name="route",
    )(plan, arrived)


def pick_kernel(place_ref, plan_ref, kept_ref, roots_ref, left_ref):
    own = plan_ref[HOME_ORIGIN + place_ref[1]] < 0

    @pl.when(own)
    def _():
        left_ref[...] = kept_ref[:, :ROWS]

    @pl.when(jnp.logical_not(own))
    def _():
        left_ref[...] = roots_ref[:, :ROWS]


def pick(place, plan, kept, roots):
    smem = pl.BlockSpec(memory_space=pltpu.SMEM)
    vmem = pl.BlockSpec(memory_space=pltpu.VMEM)
    return pl.pallas_call(
        pick_kernel,
        in_specs=[smem, smem, vmem, vmem],
        out_specs=vmem,
        out_shape=jax.ShapeDtypeStruct((kept.shape[0], ROWS, LANES), BF16),
        compiler_params=params(8),
        name="pick",
    )(place, plan, kept, roots)


def hold_kernel(place_ref, plan_ref, before_ref, kept_ref, roots_ref, both_hbm, sem):
    del before_ref
    own = plan_ref[HOME_ORIGIN + place_ref[1]] < 0

    @pl.when(own)
    def _():
        copy = pltpu.make_async_copy(kept_ref, both_hbm, sem)
        copy.start()
        copy.wait()

    @pl.when(jnp.logical_not(own))
    def _():
        copy = pltpu.make_async_copy(roots_ref, both_hbm, sem)
        copy.start()
        copy.wait()


def hold(place, plan, before, kept, roots):
    smem = pl.BlockSpec(memory_space=pltpu.SMEM)
    anywhere = pl.BlockSpec(memory_space=pl.ANY)
    return pl.pallas_call(
        hold_kernel,
        in_specs=[smem, smem, anywhere, anywhere, anywhere],
        out_specs=pl.BlockSpec(memory_space=pltpu.HBM),
        out_shape=pltpu.HBM(kept.shape, BF16),
        scratch_shapes=[pltpu.SemaphoreType.DMA],
        compiler_params=params(4),
        name="hold",
    )(place, plan, before, kept, roots)


def gather_kernel(plan_ref, gradient_ref, out_ref):
    for home in range(out_ref.shape[0]):
        out_ref[home] = gradient_ref[plan_ref[HOME_BLOCK + home]]


def gather(plan, gradient):
    return pl.pallas_call(
        gather_kernel,
        in_specs=[
            pl.BlockSpec(memory_space=pltpu.SMEM),
            pl.BlockSpec(memory_space=pltpu.VMEM),
        ],
        out_shape=jax.ShapeDtypeStruct(gradient.shape, BF16),
        compiler_params=params(8),
        name="gather",
    )(plan, gradient)


def block_kernel(rep_ref, block_hbm, both_hbm, *refs):
    shares, (out_ref, own_ref, block_ref, both_ref, left_ref, sems) = refs[:-6], refs[-6:]
    pieces, rows, order = block_ref.shape
    width = LANES
    replicas = order // width
    rep = rep_ref[0]
    roots = pltpu.make_async_copy(both_hbm, both_ref, sems.at[0])
    roots.start()
    parts = 4
    blocks = []
    for part in range(parts):
        lines = pl.ds(part * (pieces // parts), pieces // parts)
        copy = pltpu.make_async_copy(
            block_hbm.at[lines], block_ref.at[lines], sems.at[1 + part]
        )
        copy.start()
        blocks.append(copy)

    def place(index, share, start):
        row, column = row_piece(index)
        lines = pl.ds(pl.multiple_of(start + row, TILE), TILE)
        left_ref[lines, column : column + width] = share[:TILE]
        left_ref[lines, column + width : column + 2 * width] = share[TILE:]

    for share, distance in zip(shares, DISTANCES[1:]):
        start = lax.rem(rep - distance + replicas, replicas) * width
        for index in range(pieces):
            place(index, share[index], start)
    roots.wait()
    for index in range(pieces):
        place(index, both_ref[index, :ROWS], rep * width)

    right_root = both_ref[:, ROWS:].reshape(order, width)
    rooted = []
    for part, copy in enumerate(blocks):
        copy.wait()
        lines = block_ref[part * (pieces // parts) : (part + 1) * (pieces // parts)]
        rooted.append(
            jnp.dot(
                lines.reshape(order // parts, order), right_root, preferred_element_type=F32
            ).astype(BF16)
        )
    rooted = jnp.concatenate(rooted, axis=0)
    precond = jnp.dot(left_ref[...], rooted, preferred_element_type=F32)
    out_ref[:, :ROWS, :] = precond.astype(BF16).reshape(pieces, rows, width)

    block = block_ref[...].reshape(order, order)
    columns = pl.multiple_of(rep * width, width)
    own_columns = block_ref[:, :, pl.ds(columns, width)].reshape(order, width)
    own_rows = block_ref[pl.ds(rep * (width // rows), width // rows)].reshape(width, order)
    left = lax.dot_general(
        own_rows, block, (((1,), (1,)), ((), ())), preferred_element_type=F32
    ).astype(BF16)
    for index in range(pieces):
        row, column = row_piece(index)
        for at, first in enumerate((column, column + width)):
            tile = left[row : row + TILE, first : first + width]
            base = ROWS + at * TILE
            out_ref[index, base : base + TILE] = tile
            own_ref[index, at * TILE : (at + 1) * TILE] = tile
    right = jnp.dot(own_columns.T, block, preferred_element_type=F32).T
    right = right.astype(BF16).reshape(pieces, rows, width)
    out_ref[:, 2 * ROWS : 3 * ROWS, :] = right
    own_ref[:, ROWS:, :] = right

    own = own_columns.astype(F32)
    lane = lax.broadcasted_iota(jnp.int32, (TILE, width), 1)
    total = jnp.zeros((TILE, width), F32)
    values = split_three(jnp.sum(precond * precond, keepdims=True))
    values += split_three(jnp.sum(own * own, keepdims=True))
    for index, value in enumerate(values):
        total = jnp.where(lane == index, value, total)
    out_ref[:, 3 * ROWS :, :] = jnp.broadcast_to(total.astype(BF16), (pieces, TILE, width))


def block_shares(rep, block, both, shares):
    pieces, _, order = block.shape
    vmem = pl.BlockSpec(memory_space=pltpu.VMEM)
    hbm = pl.BlockSpec(memory_space=pltpu.HBM)
    return pl.pallas_call(
        block_kernel,
        in_specs=[pl.BlockSpec(memory_space=pltpu.SMEM), hbm, hbm] + [vmem] * len(shares),
        out_specs=[vmem, vmem],
        out_shape=[
            jax.ShapeDtypeStruct((pieces, 3 * ROWS + TILE, LANES), BF16),
            jax.ShapeDtypeStruct((pieces, 2 * ROWS, LANES), BF16),
        ],
        scratch_shapes=[
            pltpu.VMEM(block.shape, BF16),
            pltpu.VMEM(both.shape, BF16),
            pltpu.VMEM((order, order), BF16),
            pltpu.SemaphoreType.DMA((5,)),
        ],
        compiler_params=params(20),
        cost_estimate=cost(8 * order * order * LANES, 6 * order * order),
        name="block_shares",
    )(rep, *in_hbm(block, both), *shares)


def named_kernel(arrived_ref, update_ref):
    count = arrived_ref.shape[0]
    line = lax.broadcasted_iota(jnp.int32, (ROWS, LANES), 0)
    sums = jnp.zeros((ROWS, LANES), F32)
    for index in range(count):
        update_ref[index] = arrived_ref[index, :ROWS, :]
        tail = arrived_ref[index, 3 * ROWS :, :].astype(F32)
        sums = jnp.where(line == index, jnp.concatenate([tail, tail], axis=0), sums)
    update_ref[count] = sums.astype(BF16)


def named(arrived):
    return pl.pallas_call(
        named_kernel,
        out_shape=jax.ShapeDtypeStruct((arrived.shape[0] + 1, ROWS, LANES), BF16),
        compiler_params=params(8),
        name="named",
    )(arrived)


def deal_kernel(plan_ref, arrived_ref, products_ref):
    spares = products_ref.shape[1] // (2 * ROWS)
    for owner in range(products_ref.shape[0]):
        for spare in range(spares):
            home = plan_ref[SPARE_HOME + owner * spares + spare]
            products_ref[owner, 2 * ROWS * spare : 2 * ROWS * (spare + 1)] = arrived_ref[
                home, ROWS : 3 * ROWS, :
            ]


def deal(plan, arrived, spares):
    shape = (arrived.shape[0], spares * 2 * ROWS, LANES)
    return pl.pallas_call(
        deal_kernel,
        in_specs=[
            pl.BlockSpec(memory_space=pltpu.SMEM),
            pl.BlockSpec(memory_space=pltpu.VMEM),
        ],
        out_shape=jax.ShapeDtypeStruct(shape, BF16),
        compiler_params=params(8),
        name="deal",
    )(plan, arrived)


def finish_kernel(rep_ref, plan_ref, *refs):
    shares, (out_hbm, out_ref, scale_ref, sems) = refs[:-4], refs[-4:]
    count, rows, order = out_ref.shape
    width = LANES
    replicas = order // width
    sums = shares[0][count].astype(F32)
    for share in shares[1:]:
        sums += share[count].astype(F32)
    lane = lax.broadcasted_iota(jnp.int32, (rows, width), 1)
    pre = jnp.sum(jnp.where(lane < 3, sums, 0.0), axis=1, keepdims=True)
    grad = jnp.sum(jnp.where((lane >= 3) & (lane < 6), sums, 0.0), axis=1, keepdims=True)
    scale = jnp.sqrt(grad) / jnp.sqrt(pre + epsilon)
    scale_ref[...] = jnp.broadcast_to(scale, (rows, width))

    def place(index, share, column):
        factor = scale_ref[pl.ds(index, 1), :]
        start = pl.multiple_of(column * width, width)
        out_ref[index, :, pl.ds(start, width)] = (share.astype(F32) * factor).astype(BF16)

    copies = []
    for index in range(count):
        for share, distance in zip(shares, DISTANCES):
            place(index, share[index], lax.rem(rep_ref[0] - distance + replicas, replicas))
        block = plan_ref[HOME_BLOCK + index]
        copies.append(pltpu.make_async_copy(out_ref.at[index], out_hbm.at[block], sems.at[index]))
        copies[-1].start()
    for copy in copies:
        copy.wait()


def finish(rep, plan, shares, count, rows, order):
    shape = (count, rows, order)
    return pl.pallas_call(
        finish_kernel,
        in_specs=[pl.BlockSpec(memory_space=pltpu.SMEM)] * 2
        + [pl.BlockSpec(memory_space=pltpu.VMEM)] * len(shares),
        out_specs=pl.BlockSpec(memory_space=pltpu.HBM),
        out_shape=jax.ShapeDtypeStruct(shape, BF16),
        scratch_shapes=[
            pltpu.VMEM(shape, BF16),
            pltpu.VMEM((count, LANES), F32),
            pltpu.SemaphoreType.DMA((count,)),
        ],
        compiler_params=params(12),
        name="finish",
    )(rep, plan, *shares)


def factor_kernel(
    plan_ref,
    place_ref,
    own_ref,
    products_ref,
    left_hbm,
    right_hbm,
    left_out,
    right_out,
    *scratch,
):
    left_ref, right_ref, left_new, right_new, held_ref, sems = scratch
    pieces = products_ref.shape[0]
    slots, order, width = right_ref.shape
    reads, writes = [], []
    for slot in range(slots):
        reads.append(
            (
                pltpu.make_async_copy(left_hbm.at[0, slot], left_ref.at[slot], sems.at[0, slot]),
                pltpu.make_async_copy(right_hbm.at[0, slot], right_ref.at[slot], sems.at[1, slot]),
            )
        )
        writes.append(
            (
                pltpu.make_async_copy(left_new.at[slot], left_out.at[0, slot], sems.at[2, slot]),
                pltpu.make_async_copy(right_new.at[slot], right_out.at[0, slot], sems.at[3, slot]),
            )
        )
        for copy in reads[slot]:
            copy.start()
    held_ref[0] = own_ref[...]
    for spare in range(slots - 1):
        held_ref[spare + 1] = products_ref[:, 2 * ROWS * spare : 2 * ROWS * (spare + 1)]
    before = jnp.int32(0)
    for slot in range(slots):
        named = plan_ref[SOURCE + place_ref[1] * slots + slot] >= 0
        weight = jnp.where(named, 1.0 - decay_rate, 0.0).astype(F32)
        for copy in reads[slot]:
            copy.wait()
        held = jnp.where(before > 0, slot, 0)
        for index in range(pieces):
            row, column = row_piece(index)
            piece = held_ref[held, index].astype(F32)
            for part in range(2):
                at = (slot, pl.ds(row, TILE), pl.ds(column + part * width, width))
                product = piece[part * TILE : (part + 1) * TILE]
                left_new[at] = decay_rate * left_ref[at] + weight * product
            at = (slot, pl.ds(ROWS * index, ROWS))
            right_new[at] = decay_rate * right_ref[at] + weight * piece[ROWS:]
        for copy in writes[slot]:
            copy.start()
        before += named.astype(jnp.int32)
    for slot in range(slots):
        for copy in writes[slot]:
            copy.wait()


def factors(plan, place, own, products, left, right):
    slots, width, order = left.shape[1:]
    hbm = pl.BlockSpec(memory_space=pltpu.HBM)
    return pl.pallas_call(
        factor_kernel,
        in_specs=[
            pl.BlockSpec(memory_space=pltpu.SMEM),
            pl.BlockSpec(memory_space=pltpu.SMEM),
            pl.BlockSpec(memory_space=pltpu.VMEM),
            pl.BlockSpec(memory_space=pltpu.VMEM),
            hbm,
            hbm,
        ],
        out_specs=[hbm, hbm],
        out_shape=[
            jax.ShapeDtypeStruct(left.shape, F32),
            jax.ShapeDtypeStruct(right.shape, F32),
        ],
        scratch_shapes=[
            pltpu.VMEM((slots, width, order), F32),
            pltpu.VMEM((slots, order, width), F32),
            pltpu.VMEM((slots, width, order), F32),
            pltpu.VMEM((slots, order, width), F32),
            pltpu.VMEM((slots,) + own.shape, BF16),
            pltpu.SemaphoreType.DMA((4, slots)),
        ],
        compiler_params=params(16),
        cost_estimate=cost(2 * slots * order * order, 5 * slots * order * order),
        name="factors",
    )(plan, place, own, products, *in_hbm(left, right))


def ring_gather(share):
    size = lax.axis_size("rep")
    owners = lax.axis_size("fsdp")

    def shift(value, by):
        return lax.ppermute(value, "rep", [(i, (i + by) % size) for i in range(size)])

    up, down = [share], [share]
    first = anchor(shift(share, 1), shift(share, -1))
    up.append(first[0])
    down.append(first[1])
    for _ in range(size // 2 - 2):
        down.append(shift(down[-1], -1))
        up.append(shift(up[-1], 1))
    even = lax.axis_index("fsdp") % 2 == 0
    passed = lax.select(even, up[1], down[1])
    pairs = [
        (owner * size + i, owner * size + (i + (-3 if owner % 2 else 3)) % size)
        for owner in range(owners)
        for i in range(size)
    ]
    return up + down[1:] + [lax.ppermute(passed, ("fsdp", "rep"), pairs)]


def anchor_kernel(*refs):
    del refs


def anchor(*arrays):
    hbm = pl.BlockSpec(memory_space=pl.ANY)
    return pl.pallas_call(
        anchor_kernel,
        in_specs=[hbm] * len(arrays),
        out_specs=[hbm] * len(arrays),
        out_shape=[jax.ShapeDtypeStruct(array.shape, array.dtype) for array in arrays],
        input_output_aliases={index: index for index in range(len(arrays))},
        compiler_params=params(4),
        cost_estimate=cost(1 << 38, 1 << 10),
        name="anchor",
    )(*arrays)


def exchange(value):
    return lax.all_to_all(value, "fsdp", split_axis=0, concat_axis=0, tiled=True)


def local(gradient, block_owner, block_slot, left_state, right_state, left_root, right_root):
    owners = lax.axis_size("fsdp")
    count, rows, order = gradient.shape
    slots = left_state.shape[1]
    rep = lax.axis_index("rep").astype(jnp.int32).reshape(1)
    place = jnp.concatenate([rep, lax.axis_index("fsdp").astype(jnp.int32).reshape(1)])
    plan = make_plan(block_owner, block_slot)

    spare = pack(left_root[0], right_root[0], owners)
    kept = keep(place, plan, left_root[0], right_root[0], owners)
    roots = exchange(route(plan, exchange(spare)))
    left = pick(place, plan, kept, roots)
    packed, left = lax.optimization_barrier((gather(plan, gradient), left))
    left_shares = ring_gather(left)
    both = hold(place, plan, left_shares[1], kept, roots)
    outgoing, own = block_shares(rep, exchange(packed), both, left_shares[1:])

    arrived = exchange(outgoing)
    products = exchange(deal(plan, arrived, slots - 1))
    left_factor, right_factor = factors(plan, place, own, products, left_state, right_state)
    shares = ring_gather(named(arrived))
    shares, left_factor, right_factor = lax.optimization_barrier(
        (shares, left_factor, right_factor)
    )
    update = finish(rep, plan, shares, count, rows, order)
    return (update, left_factor, right_factor)


def solution(mesh):
    in_specs = (
        P(None, "fsdp", None),
        P(),
        P(),
        P("fsdp", None, "rep", None),
        P("fsdp", None, None, "rep"),
        P("fsdp", None, "rep", None),
        P("fsdp", None, None, "rep"),
    )
    out_specs = (P(None, "fsdp", None), P("fsdp", None, "rep", None), P("fsdp", None, None, "rep"))
    return jax.shard_map(local, mesh=mesh, in_specs=in_specs, out_specs=out_specs, check_vma=False)
```

```python
import jax
import jax.numpy as jnp
from jax import lax
from jax.experimental import pallas as pl
from jax.experimental.pallas import tpu as pltpu
from jax.sharding import PartitionSpec as P

decay_rate = 0.95
epsilon = 1e-06

F32 = jnp.float32
BF16 = jnp.bfloat16
ROWS = 32
TILE = 16
LANES = 128
DISTANCES = (0, 1, 2, 3, -1, -2, -3, 4)


def params(mebibytes):
    return pltpu.CompilerParams(vmem_limit_bytes=mebibytes * 1024 * 1024)


def in_hbm(*arrays):
    return [pltpu.with_memory_space_constraint(array, pltpu.HBM) for array in arrays]


def cost(flops, accessed):
    return pl.CostEstimate(flops=flops, bytes_accessed=accessed, transcendentals=0)


def whole(shape):
    return pl.BlockSpec(shape, lambda *_: (0,) * len(shape))


def row_piece(index):
    per_line = 1024 // (2 * LANES)
    return TILE * (index // per_line), 2 * LANES * (index % per_line)


def split_three(value):
    high = value.astype(BF16).astype(F32)
    rest = value - high
    middle = rest.astype(BF16).astype(F32)
    return high, middle, (rest - middle).astype(BF16).astype(F32)


SOURCE = 0
HOME_BLOCK = 96
HOME_ORIGIN = 128
SPARE_HOME = 160
PLAN = 256


def plan_kernel(owner_ref, slot_ref, plan_ref, list_ref):
    owners = HOME_ORIGIN - HOME_BLOCK
    slots = (HOME_BLOCK - SOURCE) // owners

    def clear(index, carry):
        plan_ref[SOURCE + index] = -1
        return carry

    def clear_spare(index, carry):
        plan_ref[SPARE_HOME + index] = 0
        return carry

    def enter(index, carry):
        plan_ref[SOURCE + owner_ref[index] * slots + slot_ref[index]] = index
        return carry

    def walk(owner, carry):
        spare, idle = carry
        count = 0
        for slot in range(slots):
            block = plan_ref[SOURCE + owner * slots + slot]
            named = block >= 0

            @pl.when(named & (count == 0))
            def _():
                plan_ref[HOME_BLOCK + owner] = block
                plan_ref[HOME_ORIGIN + owner] = -1

            @pl.when(named & (count > 0))
            def _():
                list_ref[0, spare] = block
                list_ref[1, spare] = owner * 2 + slot - 1

            spare += (named & (count > 0)).astype(jnp.int32)
            count += named.astype(jnp.int32)

        @pl.when(count == 0)
        def _():
            list_ref[2, idle] = owner

        return spare, idle + (count == 0).astype(jnp.int32)

    def assign(index, carry):
        home = list_ref[2, index]
        origin = list_ref[1, index]
        plan_ref[HOME_BLOCK + home] = list_ref[0, index]
        plan_ref[HOME_ORIGIN + home] = origin
        plan_ref[SPARE_HOME + origin] = home
        return carry

    zero = jnp.int32(0)
    lax.fori_loop(0, owners * slots, clear, zero)
    lax.fori_loop(0, 2 * owners, clear_spare, zero)
    lax.fori_loop(0, owner_ref.shape[0], enter, zero)
    _, idle = lax.fori_loop(0, owners, walk, (zero, zero))
    lax.fori_loop(0, idle, assign, zero)


def make_plan(owner, slot):
    smem = pl.BlockSpec(memory_space=pltpu.SMEM)
    return pl.pallas_call(
        plan_kernel,
        in_specs=[smem, smem],
        out_specs=smem,
        out_shape=jax.ShapeDtypeStruct((PLAN,), jnp.int32),
        scratch_shapes=[pltpu.SMEM((3, 32), jnp.int32)],
        compiler_params=params(4),
        name="make_plan",
    )(owner, slot)


def cut(left_ref, right_ref, slot, out_ref, base):
    for index in range(out_ref.shape[0]):
        row, column = row_piece(index)
        rows = pl.ds(row, TILE)
        out_ref[index, base : base + TILE] = left_ref[slot, rows, column : column + LANES]
        out_ref[index, base + TILE : base + ROWS] = left_ref[
            slot, rows, column + LANES : column + 2 * LANES
        ]
        out_ref[index, base + ROWS : base + 2 * ROWS] = right_ref[
            slot, ROWS * index : ROWS * (index + 1)
        ]


def pack_kernel(left_hbm, right_hbm, spare_hbm, left_ref, right_ref, spare_ref, sems):
    reads, writes = [], []
    for spare in range(left_ref.shape[0]):
        pair = (
            pltpu.make_async_copy(left_hbm.at[spare + 1], left_ref.at[spare], sems.at[0, spare]),
            pltpu.make_async_copy(right_hbm.at[spare + 1], right_ref.at[spare], sems.at[1, spare]),
        )
        for copy in pair:
            copy.start()
        reads.append(pair)
    for spare, pair in enumerate(reads):
        for copy in pair:
            copy.wait()
        cut(left_ref, right_ref, spare, spare_ref, 2 * ROWS * spare)
        part = (slice(None), pl.ds(2 * ROWS * spare, 2 * ROWS))
        copy = pltpu.make_async_copy(spare_ref.at[part], spare_hbm.at[part], sems.at[2, spare])
        copy.start()
        writes.append(copy)
    for copy in writes:
        copy.wait()


def pack(left, right, pieces):
    hbm = pl.BlockSpec(memory_space=pltpu.HBM)
    spares = left.shape[0] - 1
    shape = (pieces, spares * 2 * ROWS, LANES)
    return pl.pallas_call(
        pack_kernel,
        in_specs=[hbm, hbm],
        out_specs=hbm,
        out_shape=pltpu.HBM(shape, BF16),
        scratch_shapes=[
            pltpu.VMEM((spares,) + left.shape[1:], BF16),
            pltpu.VMEM((spares,) + right.shape[1:], BF16),
            pltpu.VMEM(shape, BF16),
            pltpu.SemaphoreType.DMA((3, spares)),
        ],
        compiler_params=params(8),
        name="pack",
    )(*in_hbm(left, right))


def keep_kernel(place_ref, plan_ref, left_hbm, right_hbm, kept_ref, left_ref, right_ref, sems):
    slots = left_hbm.shape[0]
    first = jnp.int32(slots - 1)
    for slot in reversed(range(slots - 1)):
        first = jnp.where(plan_ref[SOURCE + place_ref[1] * slots + slot] >= 0, slot, first)
    copies = (
        pltpu.make_async_copy(left_hbm.at[first], left_ref.at[0], sems.at[0]),
        pltpu.make_async_copy(right_hbm.at[first], right_ref.at[0], sems.at[1]),
    )
    for copy in copies:
        copy.start()
    for copy in copies:
        copy.wait()
    cut(left_ref, right_ref, 0, kept_ref, 0)


def keep(place, plan, left, right, pieces):
    smem = pl.BlockSpec(memory_space=pltpu.SMEM)
    hbm = pl.BlockSpec(memory_space=pltpu.HBM)
    return pl.pallas_call(
        keep_kernel,
        in_specs=[smem, smem, hbm, hbm],
        out_specs=pl.BlockSpec(memory_space=pltpu.VMEM),
        out_shape=jax.ShapeDtypeStruct((pieces, 2 * ROWS, LANES), BF16),
        scratch_shapes=[
            pltpu.VMEM((1,) + left.shape[1:], BF16),
            pltpu.VMEM((1,) + right.shape[1:], BF16),
            pltpu.SemaphoreType.DMA((2,)),
        ],
        compiler_params=params(8),
        name="keep",
    )(place, plan, *in_hbm(left, right))


def route_kernel(plan_ref, arrived_ref, out_hbm, out_ref, sems):
    homes = out_ref.shape[0]
    parts = sems.shape[0]
    copies = []
    for part in range(parts):
        lines = pl.ds(part * (homes // parts), homes // parts)
        for home in range(part * (homes // parts), (part + 1) * (homes // parts)):
            origin = jnp.maximum(plan_ref[HOME_ORIGIN + home], 0)
            start = pl.multiple_of(lax.rem(origin, 2) * (2 * ROWS), 2 * ROWS)
            out_ref[home] = arrived_ref[lax.div(origin, 2), pl.ds(start, 2 * ROWS), :]
        copies.append(pltpu.make_async_copy(out_ref.at[lines], out_hbm.at[lines], sems.at[part]))
        copies[-1].start()
    for copy in copies:
        copy.wait()


def route(plan, arrived):
    shape = (arrived.shape[0], 2 * ROWS, LANES)
    return pl.pallas_call(
        route_kernel,
        in_specs=[
            pl.BlockSpec(memory_space=pltpu.SMEM),
            pl.BlockSpec(memory_space=pltpu.VMEM),
        ],
        out_specs=pl.BlockSpec(memory_space=pltpu.HBM),
        out_shape=pltpu.HBM(shape, BF16),
        scratch_shapes=[pltpu.VMEM(shape, BF16), pltpu.SemaphoreType.DMA((4,))],
        compiler_params=params(8),
        name="route",
    )(plan, arrived)


def pick_kernel(place_ref, plan_ref, kept_ref, roots_ref, left_ref):
    own = plan_ref[HOME_ORIGIN + place_ref[1]] < 0

    @pl.when(own)
    def _():
        left_ref[...] = kept_ref[:, :ROWS]

    @pl.when(jnp.logical_not(own))
    def _():
        left_ref[...] = roots_ref[:, :ROWS]


def pick(place, plan, kept, roots):
    smem = pl.BlockSpec(memory_space=pltpu.SMEM)
    vmem = pl.BlockSpec(memory_space=pltpu.VMEM)
    return pl.pallas_call(
        pick_kernel,
        in_specs=[smem, smem, vmem, vmem],
        out_specs=vmem,
        out_shape=jax.ShapeDtypeStruct((kept.shape[0], ROWS, LANES), BF16),
        compiler_params=params(8),
        name="pick",
    )(place, plan, kept, roots)


def hold_kernel(place_ref, plan_ref, before_ref, kept_ref, roots_ref, both_hbm, sem):
    del before_ref
    own = plan_ref[HOME_ORIGIN + place_ref[1]] < 0

    @pl.when(own)
    def _():
        copy = pltpu.make_async_copy(kept_ref, both_hbm, sem)
        copy.start()
        copy.wait()

    @pl.when(jnp.logical_not(own))
    def _():
        copy = pltpu.make_async_copy(roots_ref, both_hbm, sem)
        copy.start()
        copy.wait()


def hold(place, plan, before, kept, roots):
    smem = pl.BlockSpec(memory_space=pltpu.SMEM)
    anywhere = pl.BlockSpec(memory_space=pl.ANY)
    return pl.pallas_call(
        hold_kernel,
        in_specs=[smem, smem, anywhere, anywhere, anywhere],
        out_specs=pl.BlockSpec(memory_space=pltpu.HBM),
        out_shape=pltpu.HBM(kept.shape, BF16),
        scratch_shapes=[pltpu.SemaphoreType.DMA],
        compiler_params=params(4),
        name="hold",
    )(place, plan, before, kept, roots)


def gather_kernel(plan_ref, gradient_ref, out_ref):
    for home in range(out_ref.shape[0]):
        out_ref[home] = gradient_ref[plan_ref[HOME_BLOCK + home]]


def gather(plan, gradient):
    return pl.pallas_call(
        gather_kernel,
        in_specs=[
            pl.BlockSpec(memory_space=pltpu.SMEM),
            pl.BlockSpec(memory_space=pltpu.VMEM),
        ],
        out_shape=jax.ShapeDtypeStruct(gradient.shape, BF16),
        compiler_params=params(8),
        name="gather",
    )(plan, gradient)


def block_kernel(rep_ref, block_hbm, both_hbm, *refs):
    shares, (out_ref, own_ref, block_ref, both_ref, left_ref, sems) = refs[:-6], refs[-6:]
    pieces, rows, order = block_ref.shape
    width = LANES
    replicas = order // width
    rep = rep_ref[0]
    roots = pltpu.make_async_copy(both_hbm, both_ref, sems.at[0])
    roots.start()
    parts = 4
    blocks = []
    for part in range(parts):
        lines = pl.ds(part * (pieces // parts), pieces // parts)
        copy = pltpu.make_async_copy(
            block_hbm.at[lines], block_ref.at[lines], sems.at[1 + part]
        )
        copy.start()
        blocks.append(copy)

    def place(index, share, start):
        row, column = row_piece(index)
        lines = pl.ds(pl.multiple_of(start + row, TILE), TILE)
        left_ref[lines, column : column + width] = share[:TILE]
        left_ref[lines, column + width : column + 2 * width] = share[TILE:]

    for share, distance in zip(shares, DISTANCES[1:]):
        start = lax.rem(rep - distance + replicas, replicas) * width
        for index in range(pieces):
            place(index, share[index], start)
    roots.wait()
    for index in range(pieces):
        place(index, both_ref[index, :ROWS], rep * width)

    right_root = both_ref[:, ROWS:].reshape(order, width)
    rooted = []
    for part, copy in enumerate(blocks):
        copy.wait()
        lines = block_ref[part * (pieces // parts) : (part + 1) * (pieces // parts)]
        rooted.append(
            jnp.dot(
                lines.reshape(order // parts, order), right_root, preferred_element_type=F32
            ).astype(BF16)
        )
    rooted = jnp.concatenate(rooted, axis=0)
    precond = jnp.dot(left_ref[...], rooted, preferred_element_type=F32)
    out_ref[:, :ROWS, :] = precond.astype(BF16).reshape(pieces, rows, width)

    block = block_ref[...].reshape(order, order)
    columns = pl.multiple_of(rep * width, width)
    own_columns = block_ref[:, :, pl.ds(columns, width)].reshape(order, width)
    own_rows = block_ref[pl.ds(rep * (width // rows), width // rows)].reshape(width, order)
    left = lax.dot_general(
        own_rows, block, (((1,), (1,)), ((), ())), preferred_element_type=F32
    ).astype(BF16)
    for index in range(pieces):
        row, column = row_piece(index)
        for at, first in enumerate((column, column + width)):
            tile = left[row : row + TILE, first : first + width]
            base = ROWS + at * TILE
            out_ref[index, base : base + TILE] = tile
            own_ref[index, at * TILE : (at + 1) * TILE] = tile
    right = jnp.dot(own_columns.T, block, preferred_element_type=F32).T
    right = right.astype(BF16).reshape(pieces, rows, width)
    out_ref[:, 2 * ROWS : 3 * ROWS, :] = right
    own_ref[:, ROWS:, :] = right

    own = own_columns.astype(F32)
    lane = lax.broadcasted_iota(jnp.int32, (TILE, width), 1)
    total = jnp.zeros((TILE, width), F32)
    values = split_three(jnp.sum(precond * precond, keepdims=True))
    values += split_three(jnp.sum(own * own, keepdims=True))
    for index, value in enumerate(values):
        total = jnp.where(lane == index, value, total)
    out_ref[:, 3 * ROWS :, :] = jnp.broadcast_to(total.astype(BF16), (pieces, TILE, width))


def block_shares(rep, block, both, shares):
    pieces, _, order = block.shape
    vmem = pl.BlockSpec(memory_space=pltpu.VMEM)
    hbm = pl.BlockSpec(memory_space=pltpu.HBM)
    return pl.pallas_call(
        block_kernel,
        in_specs=[pl.BlockSpec(memory_space=pltpu.SMEM), hbm, hbm] + [vmem] * len(shares),
        out_specs=[vmem, vmem],
        out_shape=[
            jax.ShapeDtypeStruct((pieces, 3 * ROWS + TILE, LANES), BF16),
            jax.ShapeDtypeStruct((pieces, 2 * ROWS, LANES), BF16),
        ],
        scratch_shapes=[
            pltpu.VMEM(block.shape, BF16),
            pltpu.VMEM(both.shape, BF16),
            pltpu.VMEM((order, order), BF16),
            pltpu.SemaphoreType.DMA((5,)),
        ],
        compiler_params=params(20),
        cost_estimate=cost(8 * order * order * LANES, 6 * order * order),
        name="block_shares",
    )(rep, *in_hbm(block, both), *shares)


def named_kernel(arrived_ref, update_ref):
    count = arrived_ref.shape[0]
    update_ref[:count] = arrived_ref[:, :ROWS, :]
    tails = arrived_ref[:, 3 * ROWS :, :].astype(F32)
    line = lax.broadcasted_iota(jnp.int32, tails.shape, 1)
    update_ref[count] = jnp.sum(jnp.where(line == 0, tails, 0.0), axis=1).astype(BF16)


def named(arrived):
    return pl.pallas_call(
        named_kernel,
        out_shape=jax.ShapeDtypeStruct((arrived.shape[0] + 1, ROWS, LANES), BF16),
        compiler_params=params(8),
        name="named",
    )(arrived)


def deal_kernel(plan_ref, arrived_ref, products_ref):
    spares = products_ref.shape[1] // (2 * ROWS)
    for owner in range(products_ref.shape[0]):
        for spare in range(spares):
            home = plan_ref[SPARE_HOME + owner * spares + spare]
            products_ref[owner, 2 * ROWS * spare : 2 * ROWS * (spare + 1)] = arrived_ref[
                home, ROWS : 3 * ROWS, :
            ]


def deal(plan, arrived, spares):
    shape = (arrived.shape[0], spares * 2 * ROWS, LANES)
    return pl.pallas_call(
        deal_kernel,
        in_specs=[
            pl.BlockSpec(memory_space=pltpu.SMEM),
            pl.BlockSpec(memory_space=pltpu.VMEM),
        ],
        out_shape=jax.ShapeDtypeStruct(shape, BF16),
        compiler_params=params(8),
        name="deal",
    )(plan, arrived)


def finish_kernel(rep_ref, plan_ref, *refs):
    shares, (out_hbm, out_ref, scale_ref, sems) = refs[:-4], refs[-4:]
    count, rows, order = out_ref.shape
    width = LANES
    replicas = order // width
    sums = shares[0][count].astype(F32)
    for share in shares[1:]:
        sums += share[count].astype(F32)
    lane = lax.broadcasted_iota(jnp.int32, (rows, width), 1)
    pre = jnp.sum(jnp.where(lane < 3, sums, 0.0), axis=1, keepdims=True)
    grad = jnp.sum(jnp.where((lane >= 3) & (lane < 6), sums, 0.0), axis=1, keepdims=True)
    scale = jnp.sqrt(grad) / jnp.sqrt(pre + epsilon)
    scale_ref[...] = jnp.broadcast_to(scale, (rows, width))

    def place(index, share, column):
        factor = scale_ref[pl.ds(index, 1), :]
        start = pl.multiple_of(column * width, width)
        out_ref[index, :, pl.ds(start, width)] = (share.astype(F32) * factor).astype(BF16)

    copies = []
    for index in range(count):
        for share, distance in zip(shares, DISTANCES):
            place(index, share[index], lax.rem(rep_ref[0] - distance + replicas, replicas))
        block = plan_ref[HOME_BLOCK + index]
        copies.append(pltpu.make_async_copy(out_ref.at[index], out_hbm.at[block], sems.at[index]))
        copies[-1].start()
    for copy in copies:
        copy.wait()


def finish(rep, plan, shares, count, rows, order):
    shape = (count, rows, order)
    return pl.pallas_call(
        finish_kernel,
        in_specs=[pl.BlockSpec(memory_space=pltpu.SMEM)] * 2
        + [pl.BlockSpec(memory_space=pltpu.VMEM)] * len(shares),
        out_specs=pl.BlockSpec(memory_space=pltpu.HBM),
        out_shape=jax.ShapeDtypeStruct(shape, BF16),
        scratch_shapes=[
            pltpu.VMEM(shape, BF16),
            pltpu.VMEM((count, LANES), F32),
            pltpu.SemaphoreType.DMA((count,)),
        ],
        compiler_params=params(12),
        name="finish",
    )(rep, plan, *shares)


def factor_kernel(
    plan_ref,
    place_ref,
    own_ref,
    products_ref,
    left_hbm,
    right_hbm,
    left_out,
    right_out,
    *scratch,
):
    left_ref, right_ref, left_new, right_new, held_ref, sems = scratch
    pieces = products_ref.shape[0]
    slots, order, width = right_ref.shape
    reads, writes = [], []
    for slot in range(slots):
        reads.append(
            (
                pltpu.make_async_copy(left_hbm.at[0, slot], left_ref.at[slot], sems.at[0, slot]),
                pltpu.make_async_copy(right_hbm.at[0, slot], right_ref.at[slot], sems.at[1, slot]),
            )
        )
        writes.append(
            (
                pltpu.make_async_copy(left_new.at[slot], left_out.at[0, slot], sems.at[2, slot]),
                pltpu.make_async_copy(right_new.at[slot], right_out.at[0, slot], sems.at[3, slot]),
            )
        )
        for copy in reads[slot]:
            copy.start()
    held_ref[0] = own_ref[...]
    for spare in range(slots - 1):
        held_ref[spare + 1] = products_ref[:, 2 * ROWS * spare : 2 * ROWS * (spare + 1)]
    before = jnp.int32(0)
    for slot in range(slots):
        named = plan_ref[SOURCE + place_ref[1] * slots + slot] >= 0
        weight = jnp.where(named, 1.0 - decay_rate, 0.0).astype(F32)
        for copy in reads[slot]:
            copy.wait()
        held = jnp.where(before > 0, slot, 0)
        for index in range(pieces):
            row, column = row_piece(index)
            piece = held_ref[held, index].astype(F32)
            for part in range(2):
                at = (slot, pl.ds(row, TILE), pl.ds(column + part * width, width))
                product = piece[part * TILE : (part + 1) * TILE]
                left_new[at] = decay_rate * left_ref[at] + weight * product
            at = (slot, pl.ds(ROWS * index, ROWS))
            right_new[at] = decay_rate * right_ref[at] + weight * piece[ROWS:]
        for copy in writes[slot]:
            copy.start()
        before += named.astype(jnp.int32)
    for slot in range(slots):
        for copy in writes[slot]:
            copy.wait()


def factors(plan, place, own, products, left, right):
    slots, width, order = left.shape[1:]
    hbm = pl.BlockSpec(memory_space=pltpu.HBM)
    return pl.pallas_call(
        factor_kernel,
        in_specs=[
            pl.BlockSpec(memory_space=pltpu.SMEM),
            pl.BlockSpec(memory_space=pltpu.SMEM),
            pl.BlockSpec(memory_space=pltpu.VMEM),
            pl.BlockSpec(memory_space=pltpu.VMEM),
            hbm,
            hbm,
        ],
        out_specs=[hbm, hbm],
        out_shape=[
            jax.ShapeDtypeStruct(left.shape, F32),
            jax.ShapeDtypeStruct(right.shape, F32),
        ],
        scratch_shapes=[
            pltpu.VMEM((slots, width, order), F32),
            pltpu.VMEM((slots, order, width), F32),
            pltpu.VMEM((slots, width, order), F32),
            pltpu.VMEM((slots, order, width), F32),
            pltpu.VMEM((slots,) + own.shape, BF16),
            pltpu.SemaphoreType.DMA((4, slots)),
        ],
        compiler_params=params(16),
        cost_estimate=cost(2 * slots * order * order, 5 * slots * order * order),
        name="factors",
    )(plan, place, own, products, *in_hbm(left, right))


def ring_gather(share):
    size = lax.axis_size("rep")
    owners = lax.axis_size("fsdp")

    def shift(value, by):
        return lax.ppermute(value, "rep", [(i, (i + by) % size) for i in range(size)])

    up, down = [share], [share]
    first = anchor(shift(share, 1), shift(share, -1))
    up.append(first[0])
    down.append(first[1])
    for _ in range(size // 2 - 2):
        down.append(shift(down[-1], -1))
        up.append(shift(up[-1], 1))
    even = lax.axis_index("fsdp") % 2 == 0
    passed = lax.select(even, up[1], down[1])
    pairs = [
        (owner * size + i, owner * size + (i + (-3 if owner % 2 else 3)) % size)
        for owner in range(owners)
        for i in range(size)
    ]
    return up + down[1:] + [lax.ppermute(passed, ("fsdp", "rep"), pairs)]


def anchor_kernel(*refs):
    del refs


def anchor(*arrays):
    hbm = pl.BlockSpec(memory_space=pl.ANY)
    return pl.pallas_call(
        anchor_kernel,
        in_specs=[hbm] * len(arrays),
        out_specs=[hbm] * len(arrays),
        out_shape=[jax.ShapeDtypeStruct(array.shape, array.dtype) for array in arrays],
        input_output_aliases={index: index for index in range(len(arrays))},
        compiler_params=params(4),
        cost_estimate=cost(1 << 38, 1 << 10),
        name="anchor",
    )(*arrays)


def exchange(value):
    return lax.all_to_all(value, "fsdp", split_axis=0, concat_axis=0, tiled=True)


def local(gradient, block_owner, block_slot, left_state, right_state, left_root, right_root):
    owners = lax.axis_size("fsdp")
    count, rows, order = gradient.shape
    slots = left_state.shape[1]
    rep = lax.axis_index("rep").astype(jnp.int32).reshape(1)
    place = jnp.concatenate([rep, lax.axis_index("fsdp").astype(jnp.int32).reshape(1)])
    plan = make_plan(block_owner, block_slot)

    spare = pack(left_root[0], right_root[0], owners)
    kept = keep(place, plan, left_root[0], right_root[0], owners)
    roots = exchange(route(plan, exchange(spare)))
    left = pick(place, plan, kept, roots)
    packed, left = lax.optimization_barrier((gather(plan, gradient), left))
    left_shares = ring_gather(left)
    both = hold(place, plan, left_shares[1], kept, roots)
    outgoing, own = block_shares(rep, exchange(packed), both, left_shares[1:])

    arrived = exchange(outgoing)
    products = exchange(deal(plan, arrived, slots - 1))
    left_factor, right_factor = factors(plan, place, own, products, left_state, right_state)
    shares = ring_gather(named(arrived))
    shares, left_factor, right_factor = lax.optimization_barrier(
        (shares, left_factor, right_factor)
    )
    update = finish(rep, plan, shares, count, rows, order)
    return (update, left_factor, right_factor)


def solution(mesh):
    in_specs = (
        P(None, "fsdp", None),
        P(),
        P(),
        P("fsdp", None, "rep", None),
        P("fsdp", None, None, "rep"),
        P("fsdp", None, "rep", None),
        P("fsdp", None, None, "rep"),
    )
    out_specs = (P(None, "fsdp", None), P("fsdp", None, "rep", None), P("fsdp", None, None, "rep"))
    return jax.shard_map(local, mesh=mesh, in_specs=in_specs, out_specs=out_specs, check_vma=False)
```

```python
import jax
import jax.numpy as jnp
from jax import lax
from jax.experimental import pallas as pl
from jax.experimental.pallas import tpu as pltpu
from jax.sharding import PartitionSpec as P

decay_rate = 0.95
epsilon = 1e-06

F32 = jnp.float32
BF16 = jnp.bfloat16
ROWS = 32
TILE = 16
LANES = 128
DISTANCES = (0, 1, 2, 3, -1, -2, -3, 4)


def params(mebibytes):
    return pltpu.CompilerParams(vmem_limit_bytes=mebibytes * 1024 * 1024)


def in_hbm(*arrays):
    return [pltpu.with_memory_space_constraint(array, pltpu.HBM) for array in arrays]


def cost(flops, accessed):
    return pl.CostEstimate(flops=flops, bytes_accessed=accessed, transcendentals=0)


def whole(shape):
    return pl.BlockSpec(shape, lambda *_: (0,) * len(shape))


def row_piece(index):
    per_line = 1024 // (2 * LANES)
    return TILE * (index // per_line), 2 * LANES * (index % per_line)


def split_three(value):
    high = value.astype(BF16).astype(F32)
    rest = value - high
    middle = rest.astype(BF16).astype(F32)
    return high, middle, (rest - middle).astype(BF16).astype(F32)


SOURCE = 0
HOME_BLOCK = 96
HOME_ORIGIN = 128
SPARE_HOME = 160
PLAN = 256


def plan_kernel(owner_ref, slot_ref, plan_ref, list_ref):
    owners = HOME_ORIGIN - HOME_BLOCK
    slots = (HOME_BLOCK - SOURCE) // owners

    def clear(index, carry):
        plan_ref[SOURCE + index] = -1
        return carry

    def clear_spare(index, carry):
        plan_ref[SPARE_HOME + index] = 0
        return carry

    def enter(index, carry):
        plan_ref[SOURCE + owner_ref[index] * slots + slot_ref[index]] = index
        return carry

    def walk(owner, carry):
        spare, idle = carry
        count = 0
        for slot in range(slots):
            block = plan_ref[SOURCE + owner * slots + slot]
            named = block >= 0

            @pl.when(named & (count == 0))
            def _():
                plan_ref[HOME_BLOCK + owner] = block
                plan_ref[HOME_ORIGIN + owner] = -1

            @pl.when(named & (count > 0))
            def _():
                list_ref[0, spare] = block
                list_ref[1, spare] = owner * 2 + slot - 1

            spare += (named & (count > 0)).astype(jnp.int32)
            count += named.astype(jnp.int32)

        @pl.when(count == 0)
        def _():
            list_ref[2, idle] = owner

        return spare, idle + (count == 0).astype(jnp.int32)

    def assign(index, carry):
        home = list_ref[2, index]
        origin = list_ref[1, index]
        plan_ref[HOME_BLOCK + home] = list_ref[0, index]
        plan_ref[HOME_ORIGIN + home] = origin
        plan_ref[SPARE_HOME + origin] = home
        return carry

    zero = jnp.int32(0)
    lax.fori_loop(0, owners * slots, clear, zero)
    lax.fori_loop(0, 2 * owners, clear_spare, zero)
    lax.fori_loop(0, owner_ref.shape[0], enter, zero)
    _, idle = lax.fori_loop(0, owners, walk, (zero, zero))
    lax.fori_loop(0, idle, assign, zero)


def make_plan(owner, slot):
    smem = pl.BlockSpec(memory_space=pltpu.SMEM)
    return pl.pallas_call(
        plan_kernel,
        in_specs=[smem, smem],
        out_specs=smem,
        out_shape=jax.ShapeDtypeStruct((PLAN,), jnp.int32),
        scratch_shapes=[pltpu.SMEM((3, 32), jnp.int32)],
        compiler_params=params(4),
        name="make_plan",
    )(owner, slot)


def cut(left_ref, slot, out_ref, base):
    for index in range(out_ref.shape[0]):
        row, column = row_piece(index)
        rows = pl.ds(row, TILE)
        out_ref[index, base : base + TILE] = left_ref[slot, rows, column : column + LANES]
        out_ref[index, base + TILE : base + ROWS] = left_ref[
            slot, rows, column + LANES : column + 2 * LANES
        ]


def pack_kernel(left_hbm, right_hbm, spare_hbm, left_ref, spare_ref, sems):
    spares = left_ref.shape[0]
    lefts, rights, writes = [], [], []
    for spare in range(spares):
        part = pl.ds(2 * ROWS * spare + ROWS, ROWS)
        lefts.append(
            pltpu.make_async_copy(left_hbm.at[spare + 1], left_ref.at[spare], sems.at[0, spare])
        )
        rights.append(
            pltpu.make_async_copy(
                right_hbm.at[spare + 1], spare_ref.at[:, part], sems.at[1, spare]
            )
        )
        lefts[spare].start()
        rights[spare].start()

    def write(first, kind, spare):
        part = (slice(None), pl.ds(first, ROWS))
        copy = pltpu.make_async_copy(spare_ref.at[part], spare_hbm.at[part], sems.at[kind, spare])
        copy.start()
        writes.append(copy)

    for spare in range(spares):
        base = 2 * ROWS * spare
        lefts[spare].wait()
        cut(left_ref, spare, spare_ref, base)
        write(base, 2, spare)
        rights[spare].wait()
        write(base + ROWS, 3, spare)
    for copy in writes:
        copy.wait()


def pack(left, right, pieces):
    hbm = pl.BlockSpec(memory_space=pltpu.HBM)
    slots = left.shape[0]
    spares = slots - 1
    shape = (pieces, spares * 2 * ROWS, LANES)
    return pl.pallas_call(
        pack_kernel,
        in_specs=[hbm, hbm],
        out_specs=hbm,
        out_shape=pltpu.HBM(shape, BF16),
        scratch_shapes=[
            pltpu.VMEM((spares,) + left.shape[1:], BF16),
            pltpu.VMEM(shape, BF16),
            pltpu.SemaphoreType.DMA((4, spares)),
        ],
        compiler_params=params(8),
        name="pack",
    )(*in_hbm(left, right.reshape(slots, pieces, ROWS, LANES)))


def keep_kernel(place_ref, plan_ref, left_hbm, right_hbm, kept_ref, left_ref, sems):
    slots = left_hbm.shape[0]
    first = jnp.int32(slots - 1)
    for slot in reversed(range(slots - 1)):
        first = jnp.where(plan_ref[SOURCE + place_ref[1] * slots + slot] >= 0, slot, first)
    copies = (
        pltpu.make_async_copy(left_hbm.at[first], left_ref.at[0], sems.at[0]),
        pltpu.make_async_copy(right_hbm.at[first], kept_ref.at[:, pl.ds(ROWS, ROWS)], sems.at[1]),
    )
    for copy in copies:
        copy.start()
    copies[0].wait()
    cut(left_ref, 0, kept_ref, 0)
    copies[1].wait()


def keep(place, plan, left, right, pieces):
    smem = pl.BlockSpec(memory_space=pltpu.SMEM)
    hbm = pl.BlockSpec(memory_space=pltpu.HBM)
    slots = left.shape[0]
    return pl.pallas_call(
        keep_kernel,
        in_specs=[smem, smem, hbm, hbm],
        out_specs=pl.BlockSpec(memory_space=pltpu.VMEM),
        out_shape=jax.ShapeDtypeStruct((pieces, 2 * ROWS, LANES), BF16),
        scratch_shapes=[
            pltpu.VMEM((1,) + left.shape[1:], BF16),
            pltpu.SemaphoreType.DMA((2,)),
        ],
        compiler_params=params(8),
        name="keep",
    )(place, plan, *in_hbm(left, right.reshape(slots, pieces, ROWS, LANES)))


def route_kernel(plan_ref, arrived_ref, out_hbm, out_ref, sems):
    homes = out_ref.shape[0]
    parts = sems.shape[0]
    copies = []
    for part in range(parts):
        lines = pl.ds(part * (homes // parts), homes // parts)
        for home in range(part * (homes // parts), (part + 1) * (homes // parts)):
            origin = jnp.maximum(plan_ref[HOME_ORIGIN + home], 0)
            start = pl.multiple_of(lax.rem(origin, 2) * (2 * ROWS), 2 * ROWS)
            out_ref[home] = arrived_ref[lax.div(origin, 2), pl.ds(start, 2 * ROWS), :]
        copies.append(pltpu.make_async_copy(out_ref.at[lines], out_hbm.at[lines], sems.at[part]))
        copies[-1].start()
    for copy in copies:
        copy.wait()


def route(plan, arrived):
    shape = (arrived.shape[0], 2 * ROWS, LANES)
    return pl.pallas_call(
        route_kernel,
        in_specs=[
            pl.BlockSpec(memory_space=pltpu.SMEM),
            pl.BlockSpec(memory_space=pltpu.VMEM),
        ],
        out_specs=pl.BlockSpec(memory_space=pltpu.HBM),
        out_shape=pltpu.HBM(shape, BF16),
        scratch_shapes=[pltpu.VMEM(shape, BF16), pltpu.SemaphoreType.DMA((4,))],
        compiler_params=params(8),
        name="route",
    )(plan, arrived)


def pick_kernel(place_ref, plan_ref, kept_ref, roots_ref, left_ref):
    own = plan_ref[HOME_ORIGIN + place_ref[1]] < 0

    @pl.when(own)
    def _():
        left_ref[...] = kept_ref[:, :ROWS]

    @pl.when(jnp.logical_not(own))
    def _():
        left_ref[...] = roots_ref[:, :ROWS]


def pick(place, plan, kept, roots):
    smem = pl.BlockSpec(memory_space=pltpu.SMEM)
    vmem = pl.BlockSpec(memory_space=pltpu.VMEM)
    return pl.pallas_call(
        pick_kernel,
        in_specs=[smem, smem, vmem, vmem],
        out_specs=vmem,
        out_shape=jax.ShapeDtypeStruct((kept.shape[0], ROWS, LANES), BF16),
        compiler_params=params(8),
        name="pick",
    )(place, plan, kept, roots)


def hold_kernel(place_ref, plan_ref, before_ref, kept_ref, roots_ref, both_hbm, sem):
    del before_ref
    own = plan_ref[HOME_ORIGIN + place_ref[1]] < 0

    @pl.when(own)
    def _():
        copy = pltpu.make_async_copy(kept_ref, both_hbm, sem)
        copy.start()
        copy.wait()

    @pl.when(jnp.logical_not(own))
    def _():
        copy = pltpu.make_async_copy(roots_ref, both_hbm, sem)
        copy.start()
        copy.wait()


def hold(place, plan, before, kept, roots):
    smem = pl.BlockSpec(memory_space=pltpu.SMEM)
    anywhere = pl.BlockSpec(memory_space=pl.ANY)
    return pl.pallas_call(
        hold_kernel,
        in_specs=[smem, smem, anywhere, anywhere, anywhere],
        out_specs=pl.BlockSpec(memory_space=pltpu.HBM),
        out_shape=pltpu.HBM(kept.shape, BF16),
        scratch_shapes=[pltpu.SemaphoreType.DMA],
        compiler_params=params(4),
        name="hold",
    )(place, plan, before, kept, roots)


def gather_kernel(plan_ref, gradient_ref, out_ref):
    for home in range(out_ref.shape[0]):
        out_ref[home] = gradient_ref[plan_ref[HOME_BLOCK + home]]


def gather(plan, gradient):
    return pl.pallas_call(
        gather_kernel,
        in_specs=[
            pl.BlockSpec(memory_space=pltpu.SMEM),
            pl.BlockSpec(memory_space=pltpu.VMEM),
        ],
        out_shape=jax.ShapeDtypeStruct(gradient.shape, BF16),
        compiler_params=params(8),
        name="gather",
    )(plan, gradient)


def block_kernel(rep_ref, block_hbm, both_hbm, *refs):
    shares, (out_ref, own_ref, block_ref, both_ref, left_ref, sems) = refs[:-6], refs[-6:]
    pieces, rows, order = block_ref.shape
    width = LANES
    replicas = order // width
    rep = rep_ref[0]
    roots = pltpu.make_async_copy(both_hbm, both_ref, sems.at[0])
    roots.start()
    parts = 4
    blocks = []
    for part in range(parts):
        lines = pl.ds(part * (pieces // parts), pieces // parts)
        copy = pltpu.make_async_copy(
            block_hbm.at[lines], block_ref.at[lines], sems.at[1 + part]
        )
        copy.start()
        blocks.append(copy)

    def place(index, share, start):
        row, column = row_piece(index)
        lines = pl.ds(pl.multiple_of(start + row, TILE), TILE)
        left_ref[lines, column : column + width] = share[:TILE]
        left_ref[lines, column + width : column + 2 * width] = share[TILE:]

    for share, distance in zip(shares, DISTANCES[1:]):
        start = lax.rem(rep - distance + replicas, replicas) * width
        for index in range(pieces):
            place(index, share[index], start)
    roots.wait()
    for index in range(pieces):
        place(index, both_ref[index, :ROWS], rep * width)

    right_root = both_ref[:, ROWS:].reshape(order, width)
    columns = pl.multiple_of(rep * width, width)
    rooted = []
    right = jnp.zeros((width, order), F32)
    for part, copy in enumerate(blocks):
        copy.wait()
        first, last = part * (pieces // parts), (part + 1) * (pieces // parts)
        lines = block_ref[first:last].reshape(order // parts, order)
        rooted.append(jnp.dot(lines, right_root, preferred_element_type=F32).astype(BF16))
        own = block_ref[first:last, :, pl.ds(columns, width)].reshape(order // parts, width)
        right += jnp.dot(own.T, lines, preferred_element_type=F32)
    rooted = jnp.concatenate(rooted, axis=0)
    precond = jnp.dot(left_ref[...], rooted, preferred_element_type=F32)
    out_ref[:, :ROWS, :] = precond.astype(BF16).reshape(pieces, rows, width)

    block = block_ref[...].reshape(order, order)
    own_columns = block_ref[:, :, pl.ds(columns, width)].reshape(order, width)
    own_rows = block_ref[pl.ds(rep * (width // rows), width // rows)].reshape(width, order)
    left = lax.dot_general(
        own_rows, block, (((1,), (1,)), ((), ())), preferred_element_type=F32
    ).astype(BF16)
    for index in range(pieces):
        row, column = row_piece(index)
        for at, first in enumerate((column, column + width)):
            tile = left[row : row + TILE, first : first + width]
            base = ROWS + at * TILE
            out_ref[index, base : base + TILE] = tile
            own_ref[index, at * TILE : (at + 1) * TILE] = tile
    right = jnp.dot(own_columns.T, block, preferred_element_type=F32).T
    right = right.astype(BF16).reshape(pieces, rows, width)
    out_ref[:, 2 * ROWS : 3 * ROWS, :] = right
    own_ref[:, ROWS:, :] = right

    own = own_columns.astype(F32)
    lane = lax.broadcasted_iota(jnp.int32, (TILE, width), 1)
    total = jnp.zeros((TILE, width), F32)
    values = split_three(jnp.sum(precond * precond, keepdims=True))
    values += split_three(jnp.sum(own * own, keepdims=True))
    for index, value in enumerate(values):
        total = jnp.where(lane == index, value, total)
    out_ref[:, 3 * ROWS :, :] = jnp.broadcast_to(total.astype(BF16), (pieces, TILE, width))


def block_shares(rep, block, both, shares):
    pieces, _, order = block.shape
    vmem = pl.BlockSpec(memory_space=pltpu.VMEM)
    hbm = pl.BlockSpec(memory_space=pltpu.HBM)
    return pl.pallas_call(
        block_kernel,
        in_specs=[pl.BlockSpec(memory_space=pltpu.SMEM), hbm, hbm] + [vmem] * len(shares),
        out_specs=[vmem, vmem],
        out_shape=[
            jax.ShapeDtypeStruct((pieces, 3 * ROWS + TILE, LANES), BF16),
            jax.ShapeDtypeStruct((pieces, 2 * ROWS, LANES), BF16),
        ],
        scratch_shapes=[
            pltpu.VMEM(block.shape, BF16),
            pltpu.VMEM(both.shape, BF16),
            pltpu.VMEM((order, order), BF16),
            pltpu.SemaphoreType.DMA((5,)),
        ],
        compiler_params=params(20),
        cost_estimate=cost(8 * order * order * LANES, 6 * order * order),
        name="block_shares",
    )(rep, *in_hbm(block, both), *shares)


def named_kernel(arrived_ref, update_ref):
    count = arrived_ref.shape[0]
    update_ref[:count] = arrived_ref[:, :ROWS, :]
    tails = arrived_ref[:, 3 * ROWS :, :].astype(F32)
    line = lax.broadcasted_iota(jnp.int32, tails.shape, 1)
    update_ref[count] = jnp.sum(jnp.where(line == 0, tails, 0.0), axis=1).astype(BF16)


def named(arrived):
    return pl.pallas_call(
        named_kernel,
        out_shape=jax.ShapeDtypeStruct((arrived.shape[0] + 1, ROWS, LANES), BF16),
        compiler_params=params(8),
        name="named",
    )(arrived)


def deal_kernel(plan_ref, arrived_ref, products_ref):
    spares = products_ref.shape[1] // (2 * ROWS)
    for owner in range(products_ref.shape[0]):
        for spare in range(spares):
            home = plan_ref[SPARE_HOME + owner * spares + spare]
            products_ref[owner, 2 * ROWS * spare : 2 * ROWS * (spare + 1)] = arrived_ref[
                home, ROWS : 3 * ROWS, :
            ]


def deal(plan, arrived, spares):
    shape = (arrived.shape[0], spares * 2 * ROWS, LANES)
    return pl.pallas_call(
        deal_kernel,
        in_specs=[
            pl.BlockSpec(memory_space=pltpu.SMEM),
            pl.BlockSpec(memory_space=pltpu.VMEM),
        ],
        out_shape=jax.ShapeDtypeStruct(shape, BF16),
        compiler_params=params(8),
        name="deal",
    )(plan, arrived)


def finish_kernel(rep_ref, plan_ref, *refs):
    shares, (out_hbm, out_ref, scale_ref, sems) = refs[:-4], refs[-4:]
    count, rows, order = out_ref.shape
    width = LANES
    replicas = order // width
    sums = shares[0][count].astype(F32)
    for share in shares[1:]:
        sums += share[count].astype(F32)
    lane = lax.broadcasted_iota(jnp.int32, (rows, width), 1)
    pre = jnp.sum(jnp.where(lane < 3, sums, 0.0), axis=1, keepdims=True)
    grad = jnp.sum(jnp.where((lane >= 3) & (lane < 6), sums, 0.0), axis=1, keepdims=True)
    scale = jnp.sqrt(grad) / jnp.sqrt(pre + epsilon)
    scale_ref[...] = jnp.broadcast_to(scale, (rows, width))

    def place(index, share, column):
        factor = scale_ref[pl.ds(index, 1), :]
        start = pl.multiple_of(column * width, width)
        out_ref[index, :, pl.ds(start, width)] = (share.astype(F32) * factor).astype(BF16)

    copies = []
    for index in range(count):
        for share, distance in zip(shares, DISTANCES):
            place(index, share[index], lax.rem(rep_ref[0] - distance + replicas, replicas))
        block = plan_ref[HOME_BLOCK + index]
        copies.append(pltpu.make_async_copy(out_ref.at[index], out_hbm.at[block], sems.at[index]))
        copies[-1].start()
    for copy in copies:
        copy.wait()


def finish(rep, plan, shares, count, rows, order):
    shape = (count, rows, order)
    return pl.pallas_call(
        finish_kernel,
        in_specs=[pl.BlockSpec(memory_space=pltpu.SMEM)] * 2
        + [pl.BlockSpec(memory_space=pltpu.VMEM)] * len(shares),
        out_specs=pl.BlockSpec(memory_space=pltpu.HBM),
        out_shape=jax.ShapeDtypeStruct(shape, BF16),
        scratch_shapes=[
            pltpu.VMEM(shape, BF16),
            pltpu.VMEM((count, LANES), F32),
            pltpu.SemaphoreType.DMA((count,)),
        ],
        compiler_params=params(12),
        name="finish",
    )(rep, plan, *shares)


def factor_kernel(
    plan_ref,
    place_ref,
    own_ref,
    products_ref,
    left_hbm,
    right_hbm,
    left_out,
    right_out,
    *scratch,
):
    left_ref, right_ref, left_new, right_new, held_ref, sems = scratch
    pieces = products_ref.shape[0]
    slots, order, width = right_ref.shape
    reads, writes = [], []
    for slot in range(slots):
        reads.append(
            (
                pltpu.make_async_copy(left_hbm.at[0, slot], left_ref.at[slot], sems.at[0, slot]),
                pltpu.make_async_copy(right_hbm.at[0, slot], right_ref.at[slot], sems.at[1, slot]),
            )
        )
        writes.append(
            (
                pltpu.make_async_copy(left_new.at[slot], left_out.at[0, slot], sems.at[2, slot]),
                pltpu.make_async_copy(right_new.at[slot], right_out.at[0, slot], sems.at[3, slot]),
            )
        )
        for copy in reads[slot]:
            copy.start()
    held_ref[0] = own_ref[...]
    for spare in range(slots - 1):
        held_ref[spare + 1] = products_ref[:, 2 * ROWS * spare : 2 * ROWS * (spare + 1)]
    before = jnp.int32(0)
    for slot in range(slots):
        named = plan_ref[SOURCE + place_ref[1] * slots + slot] >= 0
        weight = jnp.where(named, 1.0 - decay_rate, 0.0).astype(F32)
        for copy in reads[slot]:
            copy.wait()
        held = jnp.where(before > 0, slot, 0)
        for index in range(pieces):
            row, column = row_piece(index)
            piece = held_ref[held, index].astype(F32)
            for part in range(2):
                at = (slot, pl.ds(row, TILE), pl.ds(column + part * width, width))
                product = piece[part * TILE : (part + 1) * TILE]
                left_new[at] = decay_rate * left_ref[at] + weight * product
            at = (slot, pl.ds(ROWS * index, ROWS))
            right_new[at] = decay_rate * right_ref[at] + weight * piece[ROWS:]
        for copy in writes[slot]:
            copy.start()
        before += named.astype(jnp.int32)
    for slot in range(slots):
        for copy in writes[slot]:
            copy.wait()


def factors(plan, place, own, products, left, right):
    slots, width, order = left.shape[1:]
    hbm = pl.BlockSpec(memory_space=pltpu.HBM)
    return pl.pallas_call(
        factor_kernel,
        in_specs=[
            pl.BlockSpec(memory_space=pltpu.SMEM),
            pl.BlockSpec(memory_space=pltpu.SMEM),
            pl.BlockSpec(memory_space=pltpu.VMEM),
            pl.BlockSpec(memory_space=pltpu.VMEM),
            hbm,
            hbm,
        ],
        out_specs=[hbm, hbm],
        out_shape=[
            jax.ShapeDtypeStruct(left.shape, F32),
            jax.ShapeDtypeStruct(right.shape, F32),
        ],
        scratch_shapes=[
            pltpu.VMEM((slots, width, order), F32),
            pltpu.VMEM((slots, order, width), F32),
            pltpu.VMEM((slots, width, order), F32),
            pltpu.VMEM((slots, order, width), F32),
            pltpu.VMEM((slots,) + own.shape, BF16),
            pltpu.SemaphoreType.DMA((4, slots)),
        ],
        compiler_params=params(16),
        cost_estimate=cost(2 * slots * order * order, 5 * slots * order * order),
        name="factors",
    )(plan, place, own, products, *in_hbm(left, right))


def ring_gather(share):
    size = lax.axis_size("rep")
    owners = lax.axis_size("fsdp")

    def shift(value, by):
        return lax.ppermute(value, "rep", [(i, (i + by) % size) for i in range(size)])

    up, down = [share], [share]
    first = anchor(shift(share, 1), shift(share, -1))
    up.append(first[0])
    down.append(first[1])
    for _ in range(size // 2 - 2):
        down.append(shift(down[-1], -1))
        up.append(shift(up[-1], 1))
    even = lax.axis_index("fsdp") % 2 == 0
    passed = lax.select(even, up[1], down[1])
    pairs = [
        (owner * size + i, owner * size + (i + (-3 if owner % 2 else 3)) % size)
        for owner in range(owners)
        for i in range(size)
    ]
    return up + down[1:] + [lax.ppermute(passed, ("fsdp", "rep"), pairs)]


def anchor_kernel(*refs):
    del refs


def anchor(*arrays):
    hbm = pl.BlockSpec(memory_space=pl.ANY)
    return pl.pallas_call(
        anchor_kernel,
        in_specs=[hbm] * len(arrays),
        out_specs=[hbm] * len(arrays),
        out_shape=[jax.ShapeDtypeStruct(array.shape, array.dtype) for array in arrays],
        input_output_aliases={index: index for index in range(len(arrays))},
        compiler_params=params(4),
        cost_estimate=cost(1 << 38, 1 << 10),
        name="anchor",
    )(*arrays)


def exchange(value):
    return lax.all_to_all(value, "fsdp", split_axis=0, concat_axis=0, tiled=True)


def local(gradient, block_owner, block_slot, left_state, right_state, left_root, right_root):
    owners = lax.axis_size("fsdp")
    count, rows, order = gradient.shape
    slots = left_state.shape[1]
    rep = lax.axis_index("rep").astype(jnp.int32).reshape(1)
    place = jnp.concatenate([rep, lax.axis_index("fsdp").astype(jnp.int32).reshape(1)])
    plan = make_plan(block_owner, block_slot)

    spare = pack(left_root[0], right_root[0], owners)
    kept = keep(place, plan, left_root[0], right_root[0], owners)
    roots = exchange(route(plan, exchange(spare)))
    left = pick(place, plan, kept, roots)
    packed, left = lax.optimization_barrier((gather(plan, gradient), left))
    left_shares = ring_gather(left)
    both = hold(place, plan, left_shares[1], kept, roots)
    outgoing, own = block_shares(rep, exchange(packed), both, left_shares[1:])

    arrived = exchange(outgoing)
    products = exchange(deal(plan, arrived, slots - 1))
    left_factor, right_factor = factors(plan, place, own, products, left_state, right_state)
    shares = ring_gather(named(arrived))
    shares, left_factor, right_factor = lax.optimization_barrier(
        (shares, left_factor, right_factor)
    )
    update = finish(rep, plan, shares, count, rows, order)
    return (update, left_factor, right_factor)


def solution(mesh):
    in_specs = (
        P(None, "fsdp", None),
        P(),
        P(),
        P("fsdp", None, "rep", None),
        P("fsdp", None, None, "rep"),
        P("fsdp", None, "rep", None),
        P("fsdp", None, None, "rep"),
    )
    out_specs = (P(None, "fsdp", None), P("fsdp", None, "rep", None), P("fsdp", None, None, "rep"))
    return jax.shard_map(local, mesh=mesh, in_specs=in_specs, out_specs=out_specs, check_vma=False)
```
